128 devices in a mesh: dp: 64 (over y, z, x), shard: 2 (over core).
Axes of the slice: x: 4, y: 4, z: 4, core: 2. Of those that a mesh axis runs over, the one named last changes fastest.
Arguments:
- tokens: bfloat16 [32768, 1024], P(('dp', 'shard')), may hold values from -24 to 24
- packed_proj: bfloat16 [1024, 3072], P(('dp', 'shard')), may hold values from -0.1875 to 0.1875
- mixer_proj: bfloat16 [1024, 1024], P(('dp', 'shard')), may hold values from -0.75 to 0.75
- expand_proj: bfloat16 [1024, 5248], P(('dp', 'shard')), may hold values from -0.1875 to 0.1875
- reduce_proj: bfloat16 [1024, 2624], P(('dp', 'shard')), may hold values from -0.125 to 0.125
- first_gain: bfloat16 [1024], P(('dp', 'shard')), may hold values from 0.25 to 1.75
- second_gain: bfloat16 [1024], P(('dp', 'shard')), may hold values from 0.25 to 1.75
- sequence_lengths: int32 [512], P(('dp', 'shard')), may hold values from 0 to 256, as said below
- cotangent: bfloat16 [32768, 1024], P(('dp', 'shard')), may hold values from -24 to 24
Outputs:
- block_output: bfloat16 [32768, 1024], P(('dp', 'shard'))
- input_grad: float32 [32768, 1024], P(('dp', 'shard'))
- packed_grad: float32 [1024, 3072], P(('dp', 'shard'))
- mixer_grad: float32 [1024, 1024], P(('dp', 'shard'))
- expand_grad: float32 [1024, 5248], P(('dp', 'shard'))
- reduce_grad: float32 [1024, 2624], P(('dp', 'shard'))
- first_gain_grad: float32 [1024], P(('dp', 'shard'))
- second_gain_grad: float32 [1024], P(('dp', 'shard'))
The draws below stay inside these ranges and needn't reach their ends.
Inputs may be any that keep to these rules, and one draw needn't show every extreme that they name: `sequence_lengths`: each aligned group of 4 entries gives the sequences of one block of 256 slots in order; their sum is at most 256 and the block's remaining slots are padding. Lengths may be 0. In every draw one block holds a single sequence of 256 tokens.
All inputs are finite; a program needn't handle non-finite values.
Results may differ from the reference program's by a relative error of at most 0.019.
Values may be sent and summed in bfloat16 or wider, within the bound.
No kernel may reach another device: no remote copies, remote signals or barrier semaphores. Data moves between devices by JAX's collectives and lax.ppermute only.
A program may use at most 192 MiB of HBM per device.

```python
from functools import partial
import jax
import jax.numpy as jnp
from jax import lax

D = 1024
H = 16
HD = 64
FF = 2624
TOK_DEV = 256
SEQS = 4
TOKENS = 32768
SLOTS = 512


def draw_sequence_lengths(key, part):
    key = jax.random.fold_in(key, 7)
    load_key, cut_key, full_key = jax.random.split(key, 3)
    device_count = SLOTS // SEQS
    places = jnp.arange(device_count, dtype=jnp.int32)
    live_loads = jax.random.randint(load_key, (device_count,), 1, TOK_DEV + 1, dtype=jnp.int32)
    chosen = jax.random.randint(full_key, (), 0, device_count, dtype=jnp.int32)
    live_loads = jnp.where(places == chosen, TOK_DEV, live_loads).astype(jnp.int32)
    cut_points = jax.random.randint(cut_key, (device_count, SEQS - 1), 0, TOK_DEV + 1, dtype=jnp.int32)
    cut_points = jnp.sort(cut_points * live_loads[:, None] // TOK_DEV, axis=1).astype(jnp.int32)
    bounds = jnp.concatenate([jnp.zeros((device_count, 1), jnp.int32), cut_points, live_loads[:, None]], axis=1)
    lengths = bounds[:, 1:] - bounds[:, :-1]
    single = jnp.zeros((SEQS,), jnp.int32).at[0].set(TOK_DEV)
    lengths = jnp.where((places == chosen)[:, None], single[None, :], lengths)
    return lengths.reshape(-1).astype(jnp.int32)


def strengthened(values, stream_key, source, target, parts, factor):
    def block_of(axis_at):
        return (jnp.arange(values.shape[axis_at]) // (values.shape[axis_at] // parts)).reshape((-1,) + (1,) * (values.ndim - 1 - axis_at))

    near = jax.random.permutation(stream_key, parts)[block_of(target)]
    other_side = (block_of(target) + parts // 2) % parts
    return jnp.where((block_of(source) == near) | (block_of(source) == other_side), factor * values, values)


def steps_of(rng, shape, pieces, low, top_value):
    level, own = 1.0, jax.random.fold_in(rng, 6)
    for axis_at, blocks in pieces:
        steps = jnp.exp(jax.random.uniform(jax.random.fold_in(own, axis_at), (blocks,), jnp.float32, low / len(pieces), top_value / len(pieces)))
        level = level * jnp.repeat(steps, shape[axis_at] // blocks).reshape([-1 if axis == axis_at else 1 for axis in range(len(shape))])
    return level


def gaussian(rng, shape, deviation, bound, cuts=(), held_as=jnp.bfloat16):
    drawn = deviation * jax.random.normal(rng, shape, jnp.float32)
    if cuts:
        drawn = drawn * steps_of(rng, shape, cuts, -0.22, 0.18)
    return jnp.clip(drawn, -bound, bound).astype(held_as)


def gaussian_with(rng, extent, width, limit, cuts, heavy, kind=jnp.bfloat16):
    array = width * jax.random.normal(rng, extent, jnp.float32)
    if cuts:
        array = array * steps_of(rng, extent, cuts, -0.22, 0.18)
    return jnp.clip(strengthened(array, jax.random.fold_in(rng, 3), *heavy), -limit, limit).astype(kind)


def setup_inputs(seed: int = 0) -> dict:
    keys = jax.random.split(jax.random.key(seed), 10)
    return {
        "tokens": gaussian_with(keys[0], (TOKENS, D), 1.0, 24.0, ((0, 128),), (0, 1, 128, 5.5)),
        "packed_proj": gaussian(keys[1], (D, 3 * D), D ** -0.5, 0.1875, ((0, 128),)),
        "mixer_proj": gaussian(keys[2], (D, D), (D // 16) ** -0.5, 0.75, ((0, 128),)),
        "expand_proj": gaussian(keys[3], (D, 2 * FF), D ** -0.5, 0.1875, ((0, 128),)),
        "reduce_proj": gaussian(keys[4], (D, FF), FF ** -0.5, 0.125, ((0, 128),)),
        "first_gain": jnp.clip(1.0 + 0.15 * jax.random.normal(keys[5], (D,), jnp.float32), 0.25, 1.75).astype(jnp.bfloat16),
        "second_gain": jnp.clip(1.0 + 0.15 * jax.random.normal(keys[6], (D,), jnp.float32), 0.25, 1.75).astype(jnp.bfloat16),
        "sequence_lengths": draw_sequence_lengths(jax.random.fold_in(keys[9], 71), 0),
        "cotangent": gaussian_with(keys[8], (TOKENS, D), 1.0, 24.0, ((0, 128),), (0, 1, 128, 5.5)),
    }


epsilon = 1e-05
rope_base = 160000.0
masked_score = -1e+30
highest = lax.Precision.HIGHEST

@jax.custom_vjp
def low(v):
    return lax.optimization_barrier(v.astype(jnp.bfloat16)).astype(jnp.float32)

@jax.custom_vjp
def low_back(v):
    return v

def low_keep(v):
    return (low(v), None)

def low_pass(kept, grad):
    return (grad,)

def back_keep(v):
    return (v, None)

def back_low(kept, grad):
    return (low(grad),)
low.defvjp(low_keep, low_pass)
low_back.defvjp(back_keep, back_low)

def token_layout(lengths, slot_count):
    places = jnp.arange(slot_count, dtype=jnp.int32)
    seq_ends = jnp.cumsum(lengths).astype(jnp.int32)
    seq_starts = (seq_ends - lengths).astype(jnp.int32)
    segment = lax.optimization_barrier(jnp.sum((places[:, None] >= seq_ends[None, :]).astype(jnp.int32), axis=1)).astype(jnp.int32)
    live_mask = places < seq_ends[-1]
    picked = (segment[:, None] == jnp.arange(lengths.shape[0], dtype=jnp.int32)[None, :]).astype(jnp.int32)
    offset = lax.optimization_barrier(jnp.sum(picked * seq_starts[None, :], axis=1)).astype(jnp.int32)
    position = jnp.where(live_mask, places - offset, 0).astype(jnp.int32)
    segment = jnp.where(live_mask, segment, lengths.shape[0] + places).astype(jnp.int32)
    return (live_mask, segment, position)

def rotary_tables(position, head_size):
    half_size = head_size // 2
    frequency = rope_base ** (-(jnp.arange(half_size, dtype=jnp.float32) * 2.0 / head_size))
    angles = position.astype(jnp.float32)[..., None] * frequency
    angles = jnp.concatenate([angles, angles], axis=-1)
    return (jnp.cos(angles), jnp.sin(angles))

def rotate(values, cosine_table, sine_table):
    half_size = values.shape[-1] // 2
    turned = jnp.concatenate([-values[..., half_size:], values[..., :half_size]], axis=-1)
    return values * cosine_table[..., None, :] + turned * sine_table[..., None, :]

def layer_norm(values, gain_vector):
    row_mean = lax.optimization_barrier(jnp.mean(values, axis=-1, keepdims=True))
    centered = values - row_mean
    row_var = lax.optimization_barrier(jnp.mean(centered * centered, axis=-1, keepdims=True))
    return centered * lax.rsqrt(row_var + epsilon) * gain_vector

def attend_group(items):
    query_rows, key_rows, value_rows, segment = items
    score_scale = query_rows.shape[-1] ** (-0.5)
    scores = jnp.einsum('qhd,khd->hqk', query_rows, key_rows, precision=highest) * score_scale
    scores = low_back(scores)
    allowed = segment[:, None] == segment[None, :]
    scores = jnp.where(allowed[None], scores, masked_score)
    row_top = lax.optimization_barrier(jnp.max(scores, axis=-1, keepdims=True))
    expd = jnp.exp(scores - row_top)
    attention = expd / lax.optimization_barrier(jnp.sum(expd, axis=-1, keepdims=True))
    return jnp.einsum('hqk,khd->qhd', low(attention), value_rows, precision=highest)

def forward(stream, packed_w, mixer_w, expand_w, reduce_w, gain_one, gain_two, live_mask, segment, cosine_table, sine_table):
    group_count = stream.shape[0]
    slot_count = stream.shape[1]
    token_count = group_count * slot_count
    flat = stream.reshape(token_count, D)
    normed_one = low(layer_norm(flat, gain_one))
    packed = low_back(jnp.dot(normed_one, packed_w, precision=highest))
    packed = packed.reshape(group_count, slot_count, 3, H, HD)
    query_rows = low(rotate(packed[:, :, 0], cosine_table, sine_table))
    key_rows = low(rotate(packed[:, :, 1], cosine_table, sine_table))
    value_rows = low(packed[:, :, 2])
    mixed_heads = lax.map(jax.checkpoint(attend_group), (query_rows, key_rows, value_rows, segment))
    mixed_heads = low(low_back(mixed_heads.reshape(token_count, D)))
    attended = low_back(jnp.dot(mixed_heads, mixer_w, precision=highest))
    residual = flat + attended
    normed_two = low(layer_norm(residual, gain_two))
    gate_up = low_back(jnp.dot(normed_two, expand_w, precision=highest))
    hidden = low(jax.nn.gelu(gate_up[:, :FF], approximate=False) * gate_up[:, FF:])
    branch = low_back(jnp.dot(hidden, reduce_w.T, precision=highest))
    return live_mask.reshape(token_count, 1).astype(jnp.float32) * (residual + branch)

def reference(tokens, packed_proj, mixer_proj, expand_proj, reduce_proj, first_gain, second_gain, sequence_lengths, cotangent):
    group_count = sequence_lengths.shape[0] // SEQS
    lengths = sequence_lengths.reshape(group_count, SEQS).astype(jnp.int32)
    live_mask, segment, position = jax.vmap(partial(token_layout, slot_count=TOK_DEV))(lengths)
    cosine_table, sine_table = rotary_tables(position, HD)
    stream = tokens.astype(jnp.float32).reshape(group_count, TOK_DEV, D)
    weights = (packed_proj.astype(jnp.float32), mixer_proj.astype(jnp.float32), expand_proj.astype(jnp.float32), reduce_proj.astype(jnp.float32), first_gain.astype(jnp.float32), second_gain.astype(jnp.float32))
    layer = partial(forward, live_mask=live_mask, segment=segment, cosine_table=cosine_table, sine_table=sine_table)
    result, pull_back = jax.vjp(layer, stream, *weights)
    grads = pull_back(cotangent.astype(jnp.float32))
    return (result.astype(jnp.bfloat16), grads[0].reshape(group_count * TOK_DEV, D), grads[1], grads[2], grads[3], grads[4], grads[5], grads[6])
```

```python
import functools

import jax
import jax.numpy as jnp
from jax import lax
from jax.experimental import pallas as pl
from jax.experimental.pallas import tpu as pltpu
from jax.sharding import Mesh
from jax.sharding import PartitionSpec as P

H = 16
HD = 64
PAIR = 2 * HD
PAIRS = H // 2
epsilon = 1e-05
rope_base = 160000.0
masked_score = -1e30
AXES = ("y", "z", "x")
ALL = ("y", "z", "x", "c")
VMEM = 60 * 1024 * 1024
bf16 = jnp.bfloat16
f32 = jnp.float32

D = 1024
FF = 2624
CHUNKS = 3
CW = 896
MIX_AT = 3 * D
GAIN_AT = 4 * D
FF_AT = 4 * D + 128
W_COLS = FF_AT + CHUNKS * 3 * CW
ROWS = 512
MIX_CUTS = ((0, 384), (384, 768), (768, 1024))
A_COLS = D + 384


def dot(a, b):
    return lax.dot_general(a, b, (((1,), (0,)), ((), ())), preferred_element_type=f32)


def dot_t(a, b):
    return lax.dot_general(a, b, (((1,), (1,)), ((), ())), preferred_element_type=f32)


def dot_first(a, b):
    return lax.dot_general(a, b, (((0,), (0,)), ((), ())), preferred_element_type=f32)


def norm_parts(values):
    centered = values - jnp.mean(values, axis=-1, keepdims=True)
    scale = lax.rsqrt(jnp.mean(centered * centered, axis=-1, keepdims=True) + epsilon)
    return centered * scale, scale


def half_swapped(v, low_half):
    return jnp.where(low_half, pltpu.roll(v, PAIR - HD // 2, 1), pltpu.roll(v, HD // 2, 1))


def pair_slice(p, at=0):
    return pl.ds(pl.multiple_of(p * PAIR + at, PAIR), PAIR)


def attend_kernel(
    tok_ref, cot_ref, seg_ref, segt_ref, cos_ref, sin_ref, perm_ref, w_ref,
    qkv_ref, prob_ref, res_ref, h2_ref, gt_ref, h1t_ref, h2t_ref, mt_ref, gtt_ref, gain_ref,
    wp, wm, wg, packed, bias, mixed, sems,
):
    copies = [
        pltpu.make_async_copy(w_ref.at[:, pl.ds(GAIN_AT, 128)], wg, sems.at[0]),
        pltpu.make_async_copy(w_ref.at[:, pl.ds(0, 3 * D)], wp, sems.at[1]),
        pltpu.make_async_copy(w_ref.at[:, pl.ds(MIX_AT, D)], wm, sems.at[2]),
    ]
    for c in copies:
        c.start()
    tokens = tok_ref[...].astype(f32)
    xhat, _ = norm_parts(tokens)
    bias[...] = jnp.where(seg_ref[...] == segt_ref[...], 0.0, masked_score)
    live = seg_ref[...] < 4
    gt = jnp.where(live, cot_ref[...].astype(f32), 0.0).astype(bf16)
    gt_ref[...] = gt
    gtt_ref[...] = dot_t(perm_ref[...], gt).astype(bf16)
    copies[0].wait()
    gains = jnp.transpose(wg[...].astype(f32))[:8]
    gain_ref[...] = gains
    h1 = (xhat * gains[0:1]).astype(bf16)
    copies[1].wait()
    packed[...] = dot(h1, wp[...])
    h1t_ref[...] = dot_t(perm_ref[...], h1).astype(bf16)
    low_half = lax.broadcasted_iota(jnp.int32, (1, PAIR), 1) % HD < HD // 2
    first = lax.broadcasted_iota(jnp.int32, (1, PAIR), 1) < HD
    zero = jnp.zeros((), bf16)

    def pair(p, carry):
        cos, sin = cos_ref[...], sin_ref[...]
        q = packed[:, pair_slice(p)]
        k = packed[:, pair_slice(p, D)]
        q = (q * cos + half_swapped(q, low_half) * sin).astype(bf16)
        k = (k * cos + half_swapped(k, low_half) * sin).astype(bf16)
        v = packed[:, pair_slice(p, 2 * D)].astype(bf16)
        qkv_ref[:, pair_slice(p)] = q
        qkv_ref[:, pair_slice(p, D)] = k
        qkv_ref[:, pair_slice(p, 2 * D)] = v
        outs = []
        for side in range(2):
            mine = first if side == 0 else jnp.logical_not(first)
            scores = dot_t(jnp.where(mine, q, zero), k) * (HD**-0.5) + bias[...]
            top = jnp.max(scores, axis=-1, keepdims=True)
            e = jnp.exp(scores - top)
            probs = e * (1.0 / jnp.sum(e, axis=-1, keepdims=True))
            prob_ref[2 * p + side] = probs
            outs.append(dot(probs.astype(bf16), v))
        mixed[:, pair_slice(p)] = jnp.where(first, outs[0], outs[1]).astype(bf16)
        return carry

    lax.fori_loop(0, PAIRS, pair, 0)
    mt_ref[...] = dot_t(perm_ref[...], mixed[...]).astype(bf16)
    copies[2].wait()
    residual = tokens + dot(mixed[...], wm[...])
    res_ref[...] = residual
    xhat2, _ = norm_parts(residual)
    h2 = (xhat2 * gains[1:2]).astype(bf16)
    h2_ref[...] = h2
    h2t_ref[...] = dot_t(perm_ref[...], h2).astype(bf16)


def gated_kernel(chunk, has_sum, *refs):
    h2_ref, gt_ref, h2t_ref, gtt_ref, w_ref = refs[:5]
    refs = refs[5:]
    if has_sum:
        branch_in, gh2_in = refs[:2]
        refs = refs[2:]
    branch_ref, gh2_ref, sib_ref, own_ref, w, gate, up, gh, hid, gg, gu, sems = refs
    base = FF_AT + chunk * 3 * CW
    copies = [
        pltpu.make_async_copy(
            w_ref.at[:, pl.ds(base + i * CW, CW)], w.at[:, pl.ds(i * CW, CW)], sems.at[i]
        )
        for i in range(3)
    ]
    for c in copies:
        c.start()
    copies[0].wait()
    gate[...] = dot(h2_ref[...], w[:, :CW])
    copies[1].wait()
    up[...] = dot(h2_ref[...], w[:, CW : 2 * CW])
    copies[2].wait()
    gh[...] = dot(gt_ref[...], w[:, 2 * CW :])
    block = 16

    def rows(i, carry):
        r = pl.ds(pl.multiple_of(i * block, block), block)
        g, u, d = gate[r, :], up[r, :], gh[r, :]
        cdf = 0.5 * (1.0 + lax.erf(g * (0.5**0.5)))
        act = g * cdf
        slope = cdf + g * (jnp.exp(-0.5 * g * g) * 0.3989422804014327)
        hid[r, :] = (act * u).astype(bf16)
        gg[r, :] = (d * u * slope).astype(bf16)
        gu[r, :] = (d * act).astype(bf16)
        return carry

    lax.fori_loop(0, gate.shape[0] // block, rows, 0)
    for to, rows_at in ((sib_ref, 0), (own_ref, ROWS)):
        h2t = h2t_ref[pl.ds(rows_at, ROWS), :]
        gtt = gtt_ref[pl.ds(rows_at, ROWS), :]
        to[:, pl.ds(0, CW)] = dot(h2t, gg[...]).astype(bf16)
        to[:, pl.ds(CW, CW)] = dot(h2t, gu[...]).astype(bf16)
        to[:, pl.ds(2 * CW, CW)] = dot(gtt, hid[...]).astype(bf16)
    branch = dot_t(hid[...], w[:, 2 * CW :])
    gh2 = dot_t(gg[...], w[:, :CW]) + dot_t(gu[...], w[:, CW : 2 * CW])
    if has_sum:
        branch = branch + branch_in[...]
        gh2 = gh2 + gh2_in[...]
    branch_ref[...] = branch
    gh2_ref[...] = gh2


def back_kernel(
    tok_ref, gt_ref, seg_ref, cos_ref, sin_ref, perm_ref, gain_ref, res_ref, branch_ref, gh2_ref,
    qkv_ref, prob_ref, h1t_ref, mt_ref, w_ref,
    out_ref, gin_ref, *rest,
):
    sibs, owns = rest[:3], rest[3:6]
    wp, wm, gr, gm, gp, sems = rest[6:]
    copies = [
        pltpu.make_async_copy(w_ref.at[:, pl.ds(MIX_AT, D)], wm, sems.at[0]),
        pltpu.make_async_copy(w_ref.at[:, pl.ds(0, 3 * D)], wp, sems.at[1]),
    ]
    for c in copies:
        c.start()
    residual = res_ref[...]
    live = seg_ref[...] < 4
    out_ref[...] = jnp.where(live, residual + branch_ref[...], 0.0).astype(bf16)
    xhat2, r2 = norm_parts(residual)
    gh2 = gh2_ref[...]
    second = jnp.sum(gh2 * xhat2, axis=0, keepdims=True)
    n = gh2 * gain_ref[1:2]
    spread = jnp.mean(n * xhat2, axis=-1, keepdims=True)
    grad_res = gt_ref[...].astype(f32) + r2 * (
        n - jnp.mean(n, axis=-1, keepdims=True) - xhat2 * spread
    )
    gr[...] = grad_res
    ga = grad_res.astype(bf16)
    copies[0].wait()
    gm[...] = dot_t(ga, wm[...]).astype(bf16)
    for half, group in ((0, sibs), (ROWS, owns)):
        mt = mt_ref[pl.ds(half, ROWS), :]
        for (lo, hi), to in zip(MIX_CUTS, group):
            to[:, pl.ds(D, hi - lo)] = dot(mt, ga[:, lo:hi]).astype(bf16)
    low_half = lax.broadcasted_iota(jnp.int32, (1, PAIR), 1) % HD < HD // 2
    first = lax.broadcasted_iota(jnp.int32, (1, PAIR), 1) < HD
    zero = jnp.zeros((), bf16)

    def pair(p, carry):
        cos, sin = cos_ref[...], sin_ref[...]
        q = qkv_ref[:, pair_slice(p)]
        k = qkv_ref[:, pair_slice(p, D)]
        v = qkv_ref[:, pair_slice(p, 2 * D)]
        g = gm[:, pair_slice(p)]
        dq, dk, dv = [], [], []
        for side in range(2):
            mine = first if side == 0 else jnp.logical_not(first)
            probs = prob_ref[2 * p + side]
            grad_probs = dot_t(jnp.where(mine, g, zero), v)
            weighted = probs * grad_probs
            delta = jnp.sum(weighted, axis=-1, keepdims=True)
            gs = (weighted - probs * delta).astype(bf16)
            dq.append(dot(gs, k))
            dk.append(dot_first(gs, q))
            dv.append(dot_first(probs.astype(bf16), g))
        dq = jnp.where(first, dq[0], dq[1]) * (HD**-0.5)
        dk = jnp.where(first, dk[0], dk[1]) * (HD**-0.5)
        dv = jnp.where(first, dv[0], dv[1])
        gp[:, pair_slice(p)] = (dq * cos - half_swapped(dq, low_half) * sin).astype(bf16)
        gp[:, pair_slice(p, D)] = (dk * cos - half_swapped(dk, low_half) * sin).astype(bf16)
        gp[:, pair_slice(p, 2 * D)] = dv.astype(bf16)
        return carry

    lax.fori_loop(0, PAIRS, pair, 0)
    for half, group in ((0, sibs), (ROWS, owns)):
        h1t = h1t_ref[pl.ds(half, ROWS), :]
        for i, to in enumerate(group):
            to[:, pl.ds(0, D)] = dot(h1t, gp[:, i * D : (i + 1) * D]).astype(bf16)
    copies[1].wait()
    gh1 = dot_t(gp[...], wp[...])
    xhat1, r1 = norm_parts(tok_ref[...].astype(f32))
    one = jnp.sum(gh1 * xhat1, axis=0, keepdims=True)
    m = gh1 * gain_ref[0:1]
    spread = jnp.mean(m * xhat1, axis=-1, keepdims=True)
    gin_ref[...] = gr[...] + r1 * (m - jnp.mean(m, axis=-1, keepdims=True) - xhat1 * spread)
    at = lax.broadcasted_iota(jnp.int32, (128, D), 0)
    both = jnp.where(at == 0, one, jnp.where(at == 1, second, 0.0)).astype(bf16)
    for half, group in ((0, sibs), (ROWS, owns)):
        group[2][:, pl.ds(D + 256, 128)] = dot_t(perm_ref[pl.ds(half, ROWS), :], both).astype(bf16)


def arr(shape, dtype):
    return jax.ShapeDtypeStruct(shape, dtype)


VSPEC = pl.BlockSpec(memory_space=pltpu.VMEM)
HSPEC = pl.BlockSpec(memory_space=pl.ANY)
PARAMS = pltpu.CompilerParams(vmem_limit_bytes=VMEM)


def token_layout(lengths, slot_count):
    places = jnp.arange(slot_count, dtype=jnp.int32)
    ends = jnp.cumsum(lengths)
    starts = ends - lengths
    segment = jnp.sum((places[:, None] >= ends[None, :]).astype(jnp.int32), axis=1)
    live = places < ends[-1]
    picked = (segment[:, None] == jnp.arange(lengths.shape[0], dtype=jnp.int32)[None, :]).astype(
        jnp.int32
    )
    position = jnp.where(live, places - jnp.sum(picked * starts[None, :], axis=1), 0)
    segment = jnp.where(live, segment, lengths.shape[0] + places)
    return segment, position


def rotary_tables(position):
    frequency = rope_base ** (-(jnp.arange(HD // 2, dtype=f32) * 2.0 / HD))
    angles = position.astype(f32)[:, None] * frequency
    cos, sin = jnp.cos(angles), jnp.sin(angles)
    return (
        jnp.concatenate([cos, cos, cos, cos], axis=-1),
        jnp.concatenate([-sin, sin, -sin, sin], axis=-1),
    )


def row_order(core):
    row = jnp.arange(D, dtype=jnp.int32)
    inner = row % ROWS
    side = jnp.where(row < ROWS, 1 - core, core)
    feature = inner // 8 * 16 + side * 8 + inner % 8
    return (feature[:, None] == jnp.arange(D, dtype=jnp.int32)[None, :]).astype(bf16)


def local_step(tokens, cotangent, lengths, core, weights):
    n = tokens.shape[0]
    segment, position = token_layout(lengths, n)
    cos, sin = rotary_tables(position)
    seg_col, seg_row = segment[:, None], segment[None, :]
    perm = row_order(core)
    qkv, probs, residual, h2, gt, h1t, h2t, mt, gtt, gains = pl.pallas_call(
        attend_kernel,
        out_shape=(
            arr((n, 3 * D), bf16), arr((H, n, n), f32), arr((n, D), f32), arr((n, D), bf16),
            arr((n, D), bf16), arr((D, n), bf16), arr((D, n), bf16), arr((D, n), bf16),
            arr((D, n), bf16), arr((8, D), f32),
        ),
        in_specs=[VSPEC] * 7 + [HSPEC],
        out_specs=(VSPEC,) * 10,
        scratch_shapes=[
            pltpu.VMEM((D, 3 * D), bf16), pltpu.VMEM((D, D), bf16), pltpu.VMEM((D, 128), bf16),
            pltpu.VMEM((n, 3 * D), f32), pltpu.VMEM((n, n), f32), pltpu.VMEM((n, D), bf16),
            pltpu.SemaphoreType.DMA((3,)),
        ],
        compiler_params=PARAMS,
        name="attend",
    )(tokens, cotangent, seg_col, seg_row, cos, sin, perm, weights)
    sums = ()
    ff_sib, ff_own = [], []
    for chunk in range(CHUNKS):
        *sums, sib, own = pl.pallas_call(
            functools.partial(gated_kernel, chunk, chunk > 0),
            out_shape=(
                arr((n, D), f32), arr((n, D), f32),
                arr((ROWS, 3 * CW), bf16), arr((ROWS, 3 * CW), bf16),
            ),
            in_specs=[VSPEC] * 4 + [HSPEC] + [VSPEC] * len(sums),
            out_specs=(VSPEC,) * 4,
            scratch_shapes=[pltpu.VMEM((D, 3 * CW), bf16)]
            + [pltpu.VMEM((n, CW), f32)] * 3
            + [pltpu.VMEM((n, CW), bf16)] * 3
            + [pltpu.SemaphoreType.DMA((3,))],
            compiler_params=PARAMS,
            name="gated",
        )(h2, gt, h2t, gtt, weights, *sums)
        ff_sib.append(sib)
        ff_own.append(own)
    branch, gh2 = sums
    block_output, input_grad, *att = pl.pallas_call(
        back_kernel,
        out_shape=(arr((n, D), bf16), arr((n, D), f32)) + (arr((ROWS, A_COLS), bf16),) * 6,
        in_specs=[VSPEC] * 14 + [HSPEC],
        out_specs=(VSPEC,) * 8,
        scratch_shapes=[
            pltpu.VMEM((D, 3 * D), bf16), pltpu.VMEM((D, D), bf16), pltpu.VMEM((n, D), f32),
            pltpu.VMEM((n, D), bf16), pltpu.VMEM((n, 3 * D), bf16), pltpu.SemaphoreType.DMA((2,)),
        ],
        compiler_params=PARAMS,
        name="back",
    )(
        tokens, gt, seg_col, cos, sin, perm, gains, residual, branch, gh2,
        qkv, probs, h1t, mt, weights,
    )
    return block_output, input_grad, ff_sib, ff_own, att[:3], att[3:]


def ring_pairs(n):
    return [(i * 2 + c, (i + 1 - 2 * c) % n * 2 + c) for i in range(n) for c in range(2)]


def onward(a, axis):
    return lax.ppermute(a, (axis, "c"), ring_pairs(lax.axis_size(axis)))


def picked(a, dim, j):
    return lax.dynamic_index_in_dim(a, jnp.mod(j, a.shape[dim]), dim, keepdims=False)


def ring_sum(a, dim, axis, last):
    step = 1 - 2 * lax.axis_index("c")
    me = lax.axis_index(axis)
    n = lax.axis_size(axis)
    current = picked(a, dim, me - step)
    for s in range(n - 1):
        current = onward(current, axis).astype(f32) + picked(a, dim, me - (s + 2) * step).astype(
            f32
        )
        if s < n - 2 or not last:
            current = current.astype(bf16)
    return current


def summed_part(sib, own, order):
    arrived = lax.ppermute(sib, "c", [(0, 1), (1, 0)])
    sizes = tuple(lax.axis_size(a) for a in AXES)
    whole = (own.astype(f32) + arrived.astype(f32)).astype(bf16).reshape(*sizes, 8, -1)
    left = list(AXES)
    for i, axis in enumerate(order):
        whole = ring_sum(whole, left.index(axis), axis, i == len(order) - 1)
        left.remove(axis)
    return whole


ORDERS = (("x", "y", "z"), ("y", "z", "x"), ("z", "x", "y"))


def body(
    tokens, packed_proj, mixer_proj, expand_proj, reduce_proj, first_gain, second_gain,
    sequence_lengths, cotangent,
):
    rows = packed_proj.shape[0]
    core = lax.axis_index("c")
    pad = CHUNKS * CW - FF
    gate, up, red = (
        jnp.pad(w, ((0, 0), (0, pad)))
        for w in (expand_proj[:, :FF], expand_proj[:, FF:], reduce_proj)
    )
    gains = jnp.pad(jnp.stack([first_gain, second_gain], axis=1), ((0, 0), (0, 126)))
    pieces = [packed_proj, mixer_proj, gains]
    for j in range(CHUNKS):
        pieces += [w[:, j * CW : (j + 1) * CW] for w in (gate, up, red)]
    shard = jnp.concatenate(pieces, axis=1)
    weights = lax.all_gather(shard, ALL, axis=0, tiled=True)
    block_output, input_grad, ff_sib, ff_own, att_sib, att_own = local_step(
        tokens, cotangent, sequence_lengths, core, weights
    )
    ff = [summed_part(s, o, order) for s, o, order in zip(ff_sib, ff_own, ORDERS)]
    att = [summed_part(s, o, order) for s, o, order in zip(att_sib, att_own, ORDERS)]
    ff = [f.reshape(rows, 3 * CW) for f in ff]
    att = [a.reshape(rows, A_COLS) for a in att]
    gate_g, up_g, red_g = (
        jnp.concatenate([f[:, i * CW : (i + 1) * CW] for f in ff], axis=1)[:, :FF]
        for i in range(3)
    )
    return (
        block_output,
        input_grad,
        jnp.concatenate([a[:, :D] for a in att], axis=1),
        jnp.concatenate([a[:, D : D + hi - lo] for a, (lo, hi) in zip(att, MIX_CUTS)], axis=1),
        jnp.concatenate([gate_g, up_g], axis=1),
        red_g,
        att[2][:, D + 256],
        att[2][:, D + 257],
    )


def solution(mesh):
    torus = Mesh(mesh.devices.reshape(4, 4, 4, 2), ALL)
    row, flat = P(ALL, None), P(ALL)
    return jax.shard_map(
        body,
        mesh=torus,
        in_specs=(row,) * 5 + (flat, flat, flat, row),
        out_specs=(row,) * 6 + (flat, flat),
        check_vma=False,
    )
```

```python
import functools

import jax
import jax.numpy as jnp
from jax import lax
from jax.experimental import pallas as pl
from jax.experimental.pallas import tpu as pltpu
from jax.sharding import Mesh
from jax.sharding import PartitionSpec as P

H = 16
HD = 64
PAIR = 2 * HD
PAIRS = H // 2
epsilon = 1e-05
rope_base = 160000.0
masked_score = -1e30
AXES = ("y", "z", "x")
ALL = ("y", "z", "x", "c")
VMEM = 60 * 1024 * 1024
bf16 = jnp.bfloat16
f32 = jnp.float32

D = 1024
FF = 2624
CHUNKS = 3
CW = 896
MIX_AT = 3 * D
GAIN_AT = 4 * D
FF_AT = 4 * D + 128
W_COLS = FF_AT + CHUNKS * 3 * CW
ROWS = 512
HEAD_CUTS = ((0, 3), (3, 6), (6, 8))
MIX_CUTS = ((0, 384), (384, 768), (768, 1024))
A_COLS = (1536, 1536, 1152)


def dot(a, b):
    return lax.dot_general(a, b, (((1,), (0,)), ((), ())), preferred_element_type=f32)


def dot_t(a, b):
    return lax.dot_general(a, b, (((1,), (1,)), ((), ())), preferred_element_type=f32)


def dot_first(a, b):
    return lax.dot_general(a, b, (((0,), (0,)), ((), ())), preferred_element_type=f32)


def norm_parts(values):
    centered = values - jnp.mean(values, axis=-1, keepdims=True)
    scale = lax.rsqrt(jnp.mean(centered * centered, axis=-1, keepdims=True) + epsilon)
    return centered * scale, scale


def half_swapped(v, low_half):
    return jnp.where(low_half, pltpu.roll(v, PAIR - HD // 2, 1), pltpu.roll(v, HD // 2, 1))


def pair_slice(p, at=0):
    return pl.ds(pl.multiple_of(p * PAIR + at, PAIR), PAIR)


def cotangent_kernel(cot_ref, seg_ref, *refs):
    perms, gt_ref, gtts = refs[:CHUNKS], refs[CHUNKS], refs[CHUNKS + 1 :]
    gt = jnp.where(seg_ref[...] < 4, cot_ref[...].astype(f32), 0.0).astype(bf16)
    gt_ref[...] = gt
    for perm, gtt in zip(perms, gtts):
        gtt[...] = dot_t(perm[...], gt).astype(bf16)


def attend_kernel(
    tok_ref, seg_ref, segt_ref, cos_ref, sin_ref, w_ref,
    qkv_ref, prob_ref, res_ref, h1_ref, h2_ref, mixed, gain_ref,
    wp, wm, wg, packed, bias, sems,
):
    copies = [
        pltpu.make_async_copy(w_ref.at[:, pl.ds(GAIN_AT, 128)], wg, sems.at[0]),
        pltpu.make_async_copy(w_ref.at[:, pl.ds(0, 3 * D)], wp, sems.at[1]),
        pltpu.make_async_copy(w_ref.at[:, pl.ds(MIX_AT, D)], wm, sems.at[2]),
    ]
    for c in copies:
        c.start()
    tokens = tok_ref[...].astype(f32)
    xhat, _ = norm_parts(tokens)
    bias[...] = jnp.where(seg_ref[...] == segt_ref[...], 0.0, masked_score)
    copies[0].wait()
    gains = jnp.transpose(wg[...].astype(f32))[:8]
    gain_ref[...] = gains
    h1 = (xhat * gains[0:1]).astype(bf16)
    h1_ref[...] = h1
    copies[1].wait()
    packed[...] = dot(h1, wp[...])
    low_half = lax.broadcasted_iota(jnp.int32, (1, PAIR), 1) % HD < HD // 2
    first = lax.broadcasted_iota(jnp.int32, (1, PAIR), 1) < HD
    zero = jnp.zeros((), bf16)

    def pair(p, carry):
        cos, sin = cos_ref[...], sin_ref[...]
        q = packed[:, pair_slice(p)]
        k = packed[:, pair_slice(p, D)]
        q = (q * cos + half_swapped(q, low_half) * sin).astype(bf16)
        k = (k * cos + half_swapped(k, low_half) * sin).astype(bf16)
        v = packed[:, pair_slice(p, 2 * D)].astype(bf16)
        qkv_ref[:, pair_slice(p)] = q
        qkv_ref[:, pair_slice(p, D)] = k
        qkv_ref[:, pair_slice(p, 2 * D)] = v
        outs = []
        for side in range(2):
            mine = first if side == 0 else jnp.logical_not(first)
            scores = dot_t(jnp.where(mine, q, zero), k) * (HD**-0.5) + bias[...]
            top = jnp.max(scores, axis=-1, keepdims=True)
            e = jnp.exp(scores - top)
            probs = e * (1.0 / jnp.sum(e, axis=-1, keepdims=True))
            prob_ref[2 * p + side] = probs
            outs.append(dot(probs.astype(bf16), v))
        mixed[:, pair_slice(p)] = jnp.where(first, outs[0], outs[1]).astype(bf16)
        return carry

    lax.fori_loop(0, PAIRS, pair, 0)
    copies[2].wait()
    residual = tokens + dot(mixed[...], wm[...])
    res_ref[...] = residual
    xhat2, _ = norm_parts(residual)
    h2_ref[...] = (xhat2 * gains[1:2]).astype(bf16)


def gated_kernel(chunk, has_sum, *refs):
    h2_ref, gt_ref, w_ref = refs[:3]
    refs = refs[3:]
    if has_sum:
        branch_in, gh2_in = refs[:2]
        refs = refs[2:]
    branch_ref, gh2_ref, hid, gg, gu, w, gate, up, gh, sems = refs
    base = FF_AT + chunk * 3 * CW
    copies = [
        pltpu.make_async_copy(
            w_ref.at[:, pl.ds(base + i * CW, CW)], w.at[:, pl.ds(i * CW, CW)], sems.at[i]
        )
        for i in range(3)
    ]
    for c in copies:
        c.start()
    copies[0].wait()
    gate[...] = dot(h2_ref[...], w[:, :CW])
    copies[1].wait()
    up[...] = dot(h2_ref[...], w[:, CW : 2 * CW])
    copies[2].wait()
    gh[...] = dot(gt_ref[...], w[:, 2 * CW :])
    block = 16

    def rows(i, carry):
        r = pl.ds(pl.multiple_of(i * block, block), block)
        g, u, d = gate[r, :], up[r, :], gh[r, :]
        cdf = 0.5 * (1.0 + lax.erf(g * (0.5**0.5)))
        act = g * cdf
        slope = cdf + g * (jnp.exp(-0.5 * g * g) * 0.3989422804014327)
        hid[r, :] = (act * u).astype(bf16)
        gg[r, :] = (d * u * slope).astype(bf16)
        gu[r, :] = (d * act).astype(bf16)
        return carry

    lax.fori_loop(0, gate.shape[0] // block, rows, 0)
    branch = dot_t(hid[...], w[:, 2 * CW :])
    gh2 = dot_t(gg[...], w[:, :CW]) + dot_t(gu[...], w[:, CW : 2 * CW])
    if has_sum:
        branch = branch + branch_in[...]
        gh2 = gh2 + gh2_in[...]
    branch_ref[...] = branch
    gh2_ref[...] = gh2


def gated_grad_kernel(hid, gg, gu, h2_ref, perm_ref, gtt_ref, sib_ref, own_ref, h2t):
    h2t[...] = dot_t(perm_ref[...], h2_ref[...]).astype(bf16)
    for to, rows_at in ((sib_ref, 0), (own_ref, ROWS)):
        rows = pl.ds(rows_at, ROWS)
        to[:, pl.ds(0, CW)] = dot(h2t[rows, :], gg[...]).astype(bf16)
        to[:, pl.ds(CW, CW)] = dot(h2t[rows, :], gu[...]).astype(bf16)
        to[:, pl.ds(2 * CW, CW)] = dot(gtt_ref[rows, :], hid[...]).astype(bf16)


def residual_kernel(
    gt_ref, seg_ref, gain_ref, res_ref, branch_ref, gh2_ref, w_ref,
    out_ref, gr, ga_ref, gm, second_ref, wm, sems,
):
    copy = pltpu.make_async_copy(w_ref.at[:, pl.ds(MIX_AT, D)], wm, sems.at[0])
    copy.start()
    residual = res_ref[...]
    live = seg_ref[...] < 4
    out_ref[...] = jnp.where(live, residual + branch_ref[...], 0.0).astype(bf16)
    xhat2, r2 = norm_parts(residual)
    gh2 = gh2_ref[...]
    second_ref[...] = jnp.broadcast_to(jnp.sum(gh2 * xhat2, axis=0, keepdims=True), (8, D))
    n = gh2 * gain_ref[1:2]
    spread = jnp.mean(n * xhat2, axis=-1, keepdims=True)
    grad_res = gt_ref[...].astype(f32) + r2 * (
        n - jnp.mean(n, axis=-1, keepdims=True) - xhat2 * spread
    )
    gr[...] = grad_res
    ga = grad_res.astype(bf16)
    ga_ref[...] = ga
    copy.wait()
    gm[...] = dot_t(ga, wm[...]).astype(bf16)


def back_kernel(part, *refs):
    cos_ref, sin_ref, gm, ga, qkv_ref, prob_ref, h1_ref, mixed_ref, perm_ref = refs[:9]
    last = part == len(HEAD_CUTS) - 1
    if last:
        tok_ref, gr, gain_ref, second_ref, w_ref, gp0, gp1 = refs[9:16]
        gin_ref, sib, own, h1t, mt, gp, wp, sems = refs[16:]
        copy = pltpu.make_async_copy(w_ref.at[:, pl.ds(0, 3 * D)], wp, sems.at[0])
        copy.start()
    else:
        gp, sib, own, h1t, mt = refs[9:]
    lo, hi = HEAD_CUTS[part]
    width = (hi - lo) * PAIR
    low_half = lax.broadcasted_iota(jnp.int32, (1, PAIR), 1) % HD < HD // 2
    first = lax.broadcasted_iota(jnp.int32, (1, PAIR), 1) < HD
    zero = jnp.zeros((), bf16)

    def pair(i, carry):
        cos, sin = cos_ref[...], sin_ref[...]
        p = i + lo
        q = qkv_ref[:, pair_slice(p)]
        k = qkv_ref[:, pair_slice(p, D)]
        v = qkv_ref[:, pair_slice(p, 2 * D)]
        g = gm[:, pair_slice(p)]
        dq, dk, dv = [], [], []
        for side in range(2):
            mine = first if side == 0 else jnp.logical_not(first)
            probs = prob_ref[2 * p + side]
            grad_probs = dot_t(jnp.where(mine, g, zero), v)
            weighted = probs * grad_probs
            delta = jnp.sum(weighted, axis=-1, keepdims=True)
            gs = (weighted - probs * delta).astype(bf16)
            dq.append(dot(gs, k))
            dk.append(dot_first(gs, q))
            dv.append(dot_first(probs.astype(bf16), g))
        dq = jnp.where(first, dq[0], dq[1]) * (HD**-0.5)
        dk = jnp.where(first, dk[0], dk[1]) * (HD**-0.5)
        dv = jnp.where(first, dv[0], dv[1])
        gp[:, pair_slice(i)] = (dq * cos - half_swapped(dq, low_half) * sin).astype(bf16)
        gp[:, pair_slice(i, width)] = (dk * cos - half_swapped(dk, low_half) * sin).astype(bf16)
        gp[:, pair_slice(i, 2 * width)] = dv.astype(bf16)
        return carry

    lax.fori_loop(0, hi - lo, pair, 0)
    mix = MIX_CUTS[part]
    h1t[...] = dot_t(perm_ref[...], h1_ref[...]).astype(bf16)
    mt[...] = dot_t(perm_ref[...], mixed_ref[...]).astype(bf16)
    for half, to in ((0, sib), (ROWS, own)):
        to[:, pl.ds(0, 3 * width)] = dot(h1t[pl.ds(half, ROWS), :], gp[...]).astype(bf16)
        mixed = dot(mt[pl.ds(half, ROWS), :], ga[:, mix[0] : mix[1]])
        to[:, pl.ds(3 * width, mix[1] - mix[0])] = mixed.astype(bf16)
    if not last:
        return
    copy.wait()
    gh1 = None
    for (at, end), g in zip(HEAD_CUTS, (gp0, gp1, gp)):
        w = (end - at) * PAIR
        for i in range(3):
            term = dot_t(g[:, i * w : (i + 1) * w], wp[:, i * D + at * PAIR : i * D + end * PAIR])
            gh1 = term if gh1 is None else gh1 + term
    xhat1, r1 = norm_parts(tok_ref[...].astype(f32))
    one = jnp.sum(gh1 * xhat1, axis=0, keepdims=True)
    m = gh1 * gain_ref[0:1]
    spread = jnp.mean(m * xhat1, axis=-1, keepdims=True)
    gin_ref[...] = gr[...] + r1 * (m - jnp.mean(m, axis=-1, keepdims=True) - xhat1 * spread)
    row = lax.broadcasted_iota(jnp.int32, (128, D), 0)
    both = jnp.where(row == 0, one, jnp.where(row == 1, second_ref[0:1], 0.0)).astype(bf16)
    for half, to in ((0, sib), (ROWS, own)):
        to[:, pl.ds(3 * width + 256, 128)] = dot_t(perm_ref[pl.ds(half, ROWS), :], both).astype(bf16)


def first_kernel(own, sib, out):
    out[...] = (own[...].astype(f32) + sib[...].astype(f32)).astype(bf16)


def add_kernel(got, *refs):
    total = got[...].astype(f32)
    for r in refs[:-1]:
        total = total + r[...].astype(f32)
    refs[-1][...] = total.astype(refs[-1].dtype)


def turn_kernel(got, own, sib, before, out, send):
    wide = before.shape[1]
    out[:, pl.ds(0, wide)] = before[...]
    total = got[...].astype(f32) + own[...].astype(f32) + sib[...].astype(f32)
    out[:, pl.ds(wide, own.shape[1])] = total.astype(bf16)
    send[...] = out[pl.ds(0, send.shape[0]), :]


def turn_last_kernel(got, held, out, send):
    total = got[...].astype(f32) + held[...].astype(f32)
    out[...] = total
    send[...] = total[: send.shape[0]].astype(bf16)


def arr(shape, dtype):
    return jax.ShapeDtypeStruct(shape, dtype)


VSPEC = pl.BlockSpec(memory_space=pltpu.VMEM)
HSPEC = pl.BlockSpec(memory_space=pl.ANY)
DMA = pltpu.SemaphoreType.DMA


class Chain:
    def __init__(self):
        self.before = None

    def __call__(self, kernel, name, us, inputs, out_shape, scratch=(), in_hbm=(), specs=None):
        count = len(inputs)
        grid = (1,) if specs else ()
        specs = specs or [HSPEC if i in in_hbm else VSPEC for i in range(count)]
        run = kernel
        if self.before is not None:
            inputs, specs = (*inputs, self.before), [*specs, HSPEC]

            def run(*refs):
                kernel(*refs[:count], *refs[count + 1 :])

        out = pl.pallas_call(
            run,
            grid=grid,
            out_shape=out_shape,
            in_specs=specs,
            out_specs=(VSPEC,) * len(out_shape),
            scratch_shapes=list(scratch),
            compiler_params=pltpu.CompilerParams(vmem_limit_bytes=VMEM),
            cost_estimate=pl.CostEstimate(
                flops=int(us * 1e13), bytes_accessed=1024, transcendentals=0
            ),
            name=name,
        )(*inputs)
        self.before = out[-1]
        return out


def token_layout(lengths, slot_count):
    places = jnp.arange(slot_count, dtype=jnp.int32)
    ends = jnp.cumsum(lengths)
    starts = ends - lengths
    segment = jnp.sum((places[:, None] >= ends[None, :]).astype(jnp.int32), axis=1)
    live = places < ends[-1]
    picked = (segment[:, None] == jnp.arange(lengths.shape[0], dtype=jnp.int32)[None, :]).astype(
        jnp.int32
    )
    position = jnp.where(live, places - jnp.sum(picked * starts[None, :], axis=1), 0)
    segment = jnp.where(live, segment, lengths.shape[0] + places)
    return segment, position


def rotary_tables(position):
    frequency = rope_base ** (-(jnp.arange(HD // 2, dtype=f32) * 2.0 / HD))
    angles = position.astype(f32)[:, None] * frequency
    cos, sin = jnp.cos(angles), jnp.sin(angles)
    return (
        jnp.concatenate([cos, cos, cos, cos], axis=-1),
        jnp.concatenate([-sin, sin, -sin, sin], axis=-1),
    )


ORDERS = (("x", "y", "z"), ("y", "z", "x"), ("z", "x", "y"))


def row_order(order):
    core = lax.axis_index("c")
    row = jnp.arange(D, dtype=jnp.int32)
    mine, inner = row >= ROWS, row % ROWS
    side = jnp.where(mine, core, 1 - core)
    step = 1 - 2 * side
    place = {}
    for axis, size in zip(order, (128, 32, 8)):
        place[axis] = (lax.axis_index(axis) + 8 - (inner // size % 4 + 1) * step) % 4
    feature = ((place["y"] * 4 + place["z"]) * 4 + place["x"]) * 16 + side * 8 + inner % 8
    return (feature[:, None] == jnp.arange(D, dtype=jnp.int32)[None, :]).astype(bf16)


def onward(a, axis):
    pairs = [(i * 2 + c, (i + 1 - 2 * c) % 4 * 2 + c) for i in range(4) for c in range(2)]
    return lax.ppermute(a, (axis, "c"), pairs)


def to_sibling(a):
    return lax.ppermute(a, "c", [(0, 1), (1, 0)])


def block(rows, cols, at):
    return pl.BlockSpec((rows, cols), lambda i: (at, 0))


class PartSum:
    def __init__(self, chain, order, sib, own, merged_with=None):
        self.chain, self.order, self.own, self.with_ff = chain, order, own, merged_with
        self.arrived = to_sibling(sib)
        self.step = 0
        self.cols = own.shape[1]
        self.got = self.result = None

    def advance(self):
        t, cols, wide = self.step, self.cols, self.cols
        self.step += 1
        axis = self.order[0 if t < 3 else 1 if t < 6 else 2]
        ahead = [block(128, cols, t)] * 2
        if t == 0:
            (out,) = self.chain(
                first_kernel, "ring", 1, (self.own, self.arrived), (arr((128, cols), bf16),), specs=ahead
            )
        elif t < 3 or t == 3 and self.with_ff is None:
            (out,) = self.chain(
                add_kernel, "ring", 1, (self.got, self.own, self.arrived),
                (arr((128, cols), bf16),), specs=[VSPEC] + ahead,
            )
            if t == 3:
                self.result = out
                return
        elif t == 3:
            ff = self.with_ff.result
            self.cols = cols = cols + ff.shape[1]
            self.held, out = self.chain(
                turn_kernel, "turn", 1, (self.got, self.own, self.arrived, ff),
                (arr((128, cols), bf16), arr((32, cols), bf16)), specs=[VSPEC] + ahead + [VSPEC],
            )
        elif t == 6:
            self.held, out = self.chain(
                turn_last_kernel, "turn_last", 1, (self.got, self.held),
                (arr((32, cols), f32), arr((8, cols), bf16)), specs=[VSPEC, block(32, cols, 3)],
            )
        else:
            rows, at = (32, t - 3) if t < 6 else (8, t - 6)
            (out,) = self.chain(
                add_kernel, "ring", 1, (self.got, self.held),
                (arr((rows, cols), f32 if t == 9 else bf16),), specs=[VSPEC, block(rows, cols, at)],
            )
            if t == 9:
                self.result = out
                return
        self.got = onward(out, axis)


PLAN = (
    "g0 d0 g1 F0 d1 g2 F1 F0 d2 r b0 F2 F1 F0 A0 b1 F2 F1 F0 A1 A0 b2 F2 F1 A2 A1 A0 F2 "
    "A1 A0 A2 A1 A2 A0 A1 A2 A0 A1 A2 A0 A1 A2 A0 A1 A2 A0 A1 A2 A0 A1 A2 A2"
)


def local_step(tokens, cotangent, lengths, weights, perms, part_sum):
    n = tokens.shape[0]
    segment, position = token_layout(lengths, n)
    cos, sin = rotary_tables(position)
    seg_col, seg_row = segment[:, None], segment[None, :]
    tile = arr((n, D), bf16)
    wide = arr((n, D), f32)
    gt, *gtts = Chain()(
        cotangent_kernel, "cotangent", 4, (cotangent, seg_col, *perms),
        (tile,) + (arr((D, n), bf16),) * CHUNKS,
    )
    chain = Chain()
    qkv, probs, residual, h1, h2, mixed, gains = chain(
        attend_kernel, "attend", 21, (tokens, seg_col, seg_row, cos, sin, weights),
        (arr((n, 3 * D), bf16), arr((H, n, n), f32), wide, tile, tile, tile, arr((8, D), f32)),
        [
            pltpu.VMEM((D, 3 * D), bf16), pltpu.VMEM((D, D), bf16), pltpu.VMEM((D, 128), bf16),
            pltpu.VMEM((n, 3 * D), f32), pltpu.VMEM((n, n), f32), DMA((3,)),
        ],
        in_hbm=(5,),
    )
    sums, hidden, gps, ff, att = (), {}, [], {}, {}
    for what, index in (name[:1] + (name[1:] or "0") for name in PLAN.split()):
        i = int(index)
        if what == "g":
            *sums, hid, gg, gu = chain(
                functools.partial(gated_kernel, i, i > 0), "gated", 8, (h2, gt, weights, *sums),
                (wide, wide) + (arr((n, CW), bf16),) * 3,
                [pltpu.VMEM((D, 3 * CW), bf16)] + [pltpu.VMEM((n, CW), f32)] * 3 + [DMA((3,))],
                in_hbm=(2,),
            )
            hidden[i] = (hid, gg, gu)
        elif what == "d":
            sib, own = chain(
                gated_grad_kernel, "gated_grad", 5, (*hidden[i], h2, perms[i], gtts[i]),
                (arr((ROWS, 3 * CW), bf16),) * 2, [pltpu.VMEM((D, n), bf16)],
            )
            ff[i] = part_sum(chain, ORDERS[i], sib, own)
        elif what == "r":
            branch, gh2 = sums
            block_output, gr, ga, gm, second = chain(
                residual_kernel, "residual", 4, (gt, seg_col, gains, residual, branch, gh2, weights),
                (tile, wide, tile, tile, arr((8, D), f32)), [pltpu.VMEM((D, D), bf16), DMA((1,))],
                in_hbm=(6,),
            )
        elif what == "b":
            width = 3 * (HEAD_CUTS[i][1] - HEAD_CUTS[i][0]) * PAIR
            common = (cos, sin, gm, ga, qkv, probs, h1, mixed, perms[i])
            pieces = (arr((ROWS, A_COLS[i]), bf16),) * 2
            kernel = functools.partial(back_kernel, i)
            turned = [pltpu.VMEM((D, n), bf16)] * 2
            if i < 2:
                gp, sib, own = chain(
                    kernel, "back", 8, common, (arr((n, width), bf16),) + pieces, turned
                )
                gps.append(gp)
            else:
                input_grad, sib, own = chain(
                    kernel, "back_last", 12, common + (tokens, gr, gains, second, weights, *gps),
                    (wide,) + pieces,
                    turned + [pltpu.VMEM((n, width), bf16), pltpu.VMEM((D, 3 * D), bf16), DMA((1,))],
                    in_hbm=(13,),
                )
            att[i] = part_sum(chain, ORDERS[i], sib, own, ff[i])
        else:
            (ff if what == "F" else att)[i].advance()
    return block_output, input_grad, ff, att


def own_rows(parts):
    ff = [p[:, : 3 * CW] for p in parts]
    att = [p[:, 3 * CW :] for p in parts]
    gate_g, up_g, red_g = (
        jnp.concatenate([f[:, i * CW : (i + 1) * CW] for f in ff], axis=1)[:, :FF]
        for i in range(3)
    )
    packed, mixer = [[], [], []], []
    for a, (lo, hi), (at, end) in zip(att, HEAD_CUTS, MIX_CUTS):
        width = (hi - lo) * PAIR
        for i in range(3):
            packed[i].append(a[:, i * width : (i + 1) * width])
        mixer.append(a[:, 3 * width : 3 * width + end - at])
    return (
        jnp.concatenate(packed[0] + packed[1] + packed[2], axis=1),
        jnp.concatenate(mixer, axis=1),
        jnp.concatenate([gate_g, up_g], axis=1),
        red_g,
        att[2][:, A_COLS[2] - 128],
        att[2][:, A_COLS[2] - 127],
    )


def body(
    tokens, packed_proj, mixer_proj, expand_proj, reduce_proj, first_gain, second_gain,
    sequence_lengths, cotangent,
):
    pad = CHUNKS * CW - FF
    gate, up, red = (
        jnp.pad(w, ((0, 0), (0, pad)))
        for w in (expand_proj[:, :FF], expand_proj[:, FF:], reduce_proj)
    )
    gains = jnp.pad(jnp.stack([first_gain, second_gain], axis=1), ((0, 0), (0, 126)))
    pieces = [packed_proj, mixer_proj, gains]
    for j in range(CHUNKS):
        pieces += [w[:, j * CW : (j + 1) * CW] for w in (gate, up, red)]
    shard = jnp.concatenate(pieces, axis=1)
    weights = lax.all_gather(shard, ALL, axis=0, tiled=True)
    perms = [row_order(order) for order in ORDERS]
    block_output, input_grad, _, att = local_step(
        tokens, cotangent, sequence_lengths, weights, perms, PartSum
    )
    return (block_output, input_grad, *own_rows([att[i].result for i in range(CHUNKS)]))


def solution(mesh):
    torus = Mesh(mesh.devices.reshape(4, 4, 4, 2), ALL)
    row, flat = P(ALL, None), P(ALL)
    return jax.shard_map(
        body,
        mesh=torus,
        in_specs=(row,) * 5 + (flat, flat, flat, row),
        out_specs=(row,) * 6 + (flat, flat),
        check_vma=False,
    )
```

```python
import functools

import jax
import jax.numpy as jnp
from jax import lax
from jax.experimental import pallas as pl
from jax.experimental.pallas import tpu as pltpu
from jax.sharding import Mesh
from jax.sharding import PartitionSpec as P

H = 16
HD = 64
PAIR = 2 * HD
PAIRS = H // 2
epsilon = 1e-05
rope_base = 160000.0
masked_score = -1e30
AXES = ("y", "z", "x")
ALL = ("y", "z", "x", "c")
VMEM = 60 * 1024 * 1024
bf16 = jnp.bfloat16
f32 = jnp.float32

D = 1024
FF = 2624
CHUNKS = 3
CW = 896
MIX_AT = 3 * D
GAIN_AT = 4 * D
FF_AT = 4 * D + 128
W_COLS = FF_AT + CHUNKS * 3 * CW
ROWS = 512
MIX_CUTS = ((0, 384), (384, 768), (768, 1024))
A_COLS = D + 384


def dot(a, b):
    return lax.dot_general(a, b, (((1,), (0,)), ((), ())), preferred_element_type=f32)


def dot_t(a, b):
    return lax.dot_general(a, b, (((1,), (1,)), ((), ())), preferred_element_type=f32)


def dot_first(a, b):
    return lax.dot_general(a, b, (((0,), (0,)), ((), ())), preferred_element_type=f32)


def norm_parts(values):
    centered = values - jnp.mean(values, axis=-1, keepdims=True)
    scale = lax.rsqrt(jnp.mean(centered * centered, axis=-1, keepdims=True) + epsilon)
    return centered * scale, scale


def half_swapped(v, low_half):
    return jnp.where(low_half, pltpu.roll(v, PAIR - HD // 2, 1), pltpu.roll(v, HD // 2, 1))


def pair_slice(p, at=0):
    return pl.ds(pl.multiple_of(p * PAIR + at, PAIR), PAIR)


def cotangent_kernel(cot_ref, seg_ref, *refs):
    perms, gt_ref, gtts = refs[:CHUNKS], refs[CHUNKS], refs[CHUNKS + 1 :]
    gt = jnp.where(seg_ref[...] < 4, cot_ref[...].astype(f32), 0.0).astype(bf16)
    gt_ref[...] = gt
    for perm, gtt in zip(perms, gtts):
        gtt[...] = dot_t(perm[...], gt).astype(bf16)


def attend_kernel(
    tok_ref, seg_ref, segt_ref, cos_ref, sin_ref, w_ref,
    qkv_ref, prob_ref, res_ref, h1_ref, h2_ref, mixed, gain_ref,
    wp, wm, wg, packed, bias, sems,
):
    copies = [
        pltpu.make_async_copy(w_ref.at[:, pl.ds(GAIN_AT, 128)], wg, sems.at[0]),
        pltpu.make_async_copy(w_ref.at[:, pl.ds(0, 3 * D)], wp, sems.at[1]),
        pltpu.make_async_copy(w_ref.at[:, pl.ds(MIX_AT, D)], wm, sems.at[2]),
    ]
    for c in copies:
        c.start()
    tokens = tok_ref[...].astype(f32)
    xhat, _ = norm_parts(tokens)
    bias[...] = jnp.where(seg_ref[...] == segt_ref[...], 0.0, masked_score)
    copies[0].wait()
    gains = jnp.transpose(wg[...].astype(f32))[:8]
    gain_ref[...] = gains
    h1 = (xhat * gains[0:1]).astype(bf16)
    h1_ref[...] = h1
    copies[1].wait()
    packed[...] = dot(h1, wp[...])
    low_half = lax.broadcasted_iota(jnp.int32, (1, PAIR), 1) % HD < HD // 2
    first = lax.broadcasted_iota(jnp.int32, (1, PAIR), 1) < HD
    zero = jnp.zeros((), bf16)

    def pair(p, carry):
        cos, sin = cos_ref[...], sin_ref[...]
        q = packed[:, pair_slice(p)]
        k = packed[:, pair_slice(p, D)]
        q = (q * cos + half_swapped(q, low_half) * sin).astype(bf16)
        k = (k * cos + half_swapped(k, low_half) * sin).astype(bf16)
        v = packed[:, pair_slice(p, 2 * D)].astype(bf16)
        qkv_ref[:, pair_slice(p)] = q
        qkv_ref[:, pair_slice(p, D)] = k
        qkv_ref[:, pair_slice(p, 2 * D)] = v
        outs = []
        for side in range(2):
            mine = first if side == 0 else jnp.logical_not(first)
            scores = dot_t(jnp.where(mine, q, zero), k) * (HD**-0.5) + bias[...]
            top = jnp.max(scores, axis=-1, keepdims=True)
            e = jnp.exp(scores - top)
            probs = e * (1.0 / jnp.sum(e, axis=-1, keepdims=True))
            prob_ref[2 * p + side] = probs
            outs.append(dot(probs.astype(bf16), v))
        mixed[:, pair_slice(p)] = jnp.where(first, outs[0], outs[1]).astype(bf16)
        return carry

    lax.fori_loop(0, PAIRS, pair, 0)
    copies[2].wait()
    residual = tokens + dot(mixed[...], wm[...])
    res_ref[...] = residual
    xhat2, _ = norm_parts(residual)
    h2_ref[...] = (xhat2 * gains[1:2]).astype(bf16)


def started(pairs, sems):
    copies = [pltpu.make_async_copy(a, b, sems.at[i]) for i, (a, b) in enumerate(pairs)]
    for c in copies:
        c.start()
    return copies


def gated_kernel(chunk, has_sum, h2_hbm, gt_hbm, perm_hbm, gtt_hbm, w_hbm, *refs):
    if has_sum:
        branch_in, gh2_in = refs[:2]
        refs = refs[2:]
    branch_ref, gh2_ref, sib_hbm, own_hbm = refs[:4]
    h2, gt, perm, gtt, w, gate, up, gh, hid, gg, gu, h2t, grads, sems, out_sems = refs[4:]
    base = FF_AT + chunk * 3 * CW
    pieces = [
        (w_hbm.at[:, pl.ds(base + i * CW, CW)], w.at[:, pl.ds(i * CW, CW)]) for i in range(3)
    ]
    copies = started(
        [(h2_hbm, h2), pieces[0], pieces[1], (gt_hbm, gt), pieces[2], (perm_hbm, perm), (gtt_hbm, gtt)],
        sems,
    )
    copies[0].wait()
    copies[1].wait()
    gate[...] = dot(h2[...], w[:, :CW])
    copies[2].wait()
    up[...] = dot(h2[...], w[:, CW : 2 * CW])
    copies[3].wait()
    copies[4].wait()
    gh[...] = dot(gt[...], w[:, 2 * CW :])
    copies[5].wait()
    h2t[...] = dot_t(perm[...], h2[...]).astype(bf16)
    size = 16

    def rows(i, carry):
        r = pl.ds(pl.multiple_of(i * size, size), size)
        g, u, d = gate[r, :], up[r, :], gh[r, :]
        cdf = 0.5 * (1.0 + lax.erf(g * (0.5**0.5)))
        act = g * cdf
        slope = cdf + g * (jnp.exp(-0.5 * g * g) * 0.3989422804014327)
        hid[r, :] = (act * u).astype(bf16)
        gg[r, :] = (d * u * slope).astype(bf16)
        gu[r, :] = (d * act).astype(bf16)
        return carry

    lax.fori_loop(0, gate.shape[0] // size, rows, 0)
    copies[6].wait()
    outs = []
    for half, to in enumerate((sib_hbm, own_hbm)):
        rows_at = pl.ds(half * ROWS, ROWS)
        for i, (left, right) in enumerate(((h2t, gg), (h2t, gu), (gtt, hid))):
            cols = pl.ds(i * CW, CW)
            grads[rows_at, cols] = dot(left[rows_at, :], right[...]).astype(bf16)
            outs.append(
                pltpu.make_async_copy(
                    grads.at[rows_at, cols], to.at[:, cols], out_sems.at[3 * half + i]
                )
            )
            outs[-1].start()
    branch = dot_t(hid[...], w[:, 2 * CW :])
    gh2 = dot_t(gg[...], w[:, :CW]) + dot_t(gu[...], w[:, CW : 2 * CW])
    if has_sum:
        branch = branch + branch_in[...]
        gh2 = gh2 + gh2_in[...]
    branch_ref[...] = branch
    gh2_ref[...] = gh2
    for c in outs:
        c.wait()


def heads_kernel(
    gt_ref, seg_ref, gain_ref, res_ref, branch_ref, gh2_ref, cos_ref, sin_ref,
    qkv_hbm, prob_hbm, w_hbm,
    out_ref, gr, ga_ref, second_ref, gp,
    wm, qkv, prob, gm, sems,
):
    copies = started(
        [(w_hbm.at[:, pl.ds(MIX_AT, D)], wm), (qkv_hbm, qkv), (prob_hbm, prob)], sems
    )
    residual = res_ref[...]
    live = seg_ref[...] < 4
    out_ref[...] = jnp.where(live, residual + branch_ref[...], 0.0).astype(bf16)
    xhat2, r2 = norm_parts(residual)
    gh2 = gh2_ref[...]
    second_ref[...] = jnp.broadcast_to(jnp.sum(gh2 * xhat2, axis=0, keepdims=True), (8, D))
    n = gh2 * gain_ref[1:2]
    spread = jnp.mean(n * xhat2, axis=-1, keepdims=True)
    grad_res = gt_ref[...].astype(f32) + r2 * (
        n - jnp.mean(n, axis=-1, keepdims=True) - xhat2 * spread
    )
    gr[...] = grad_res
    ga = grad_res.astype(bf16)
    ga_ref[...] = ga
    copies[0].wait()
    gm[...] = dot_t(ga, wm[...]).astype(bf16)
    copies[1].wait()
    copies[2].wait()
    low_half = lax.broadcasted_iota(jnp.int32, (1, PAIR), 1) % HD < HD // 2
    first = lax.broadcasted_iota(jnp.int32, (1, PAIR), 1) < HD
    zero = jnp.zeros((), bf16)

    def pair(p, carry):
        cos, sin = cos_ref[...], sin_ref[...]
        q = qkv[:, pair_slice(p)]
        k = qkv[:, pair_slice(p, D)]
        v = qkv[:, pair_slice(p, 2 * D)]
        g = gm[:, pair_slice(p)]
        dq, dk, dv = [], [], []
        for side in range(2):
            mine = first if side == 0 else jnp.logical_not(first)
            probs = prob[2 * p + side]
            grad_probs = dot_t(jnp.where(mine, g, zero), v)
            weighted = probs * grad_probs
            delta = jnp.sum(weighted, axis=-1, keepdims=True)
            gs = (weighted - probs * delta).astype(bf16)
            dq.append(dot(gs, k))
            dk.append(dot_first(gs, q))
            dv.append(dot_first(probs.astype(bf16), g))
        dq = jnp.where(first, dq[0], dq[1]) * (HD**-0.5)
        dk = jnp.where(first, dk[0], dk[1]) * (HD**-0.5)
        dv = jnp.where(first, dv[0], dv[1])
        gp[:, pair_slice(p)] = (dq * cos - half_swapped(dq, low_half) * sin).astype(bf16)
        gp[:, pair_slice(p, D)] = (dk * cos - half_swapped(dk, low_half) * sin).astype(bf16)
        gp[:, pair_slice(p, 2 * D)] = dv.astype(bf16)
        return carry

    lax.fori_loop(0, PAIRS, pair, 0)


def back_kernel(
    h1_ref, mixed_ref, ga, gp, tok_ref, gr, gain_ref, second_ref, perm0, perm1, perm2, w_hbm,
    gin_ref, sib0, sib1, sib2, own0, own1, own2,
    p0, p1, p2, wp, h1t, mt, grads, sems, out_sems,
):
    perms = (p0, p1, p2)
    copies = started(
        [(perm0, p0), (perm1, p1), (perm2, p2), (w_hbm.at[:, pl.ds(0, 3 * D)], wp)], sems
    )
    outs = []
    for j in range(CHUNKS):
        copies[j].wait()
        h1t[...] = dot_t(perms[j][...], h1_ref[...]).astype(bf16)
        mt[...] = dot_t(perms[j][...], mixed_ref[...]).astype(bf16)
        lo, hi = MIX_CUTS[j]
        to = grads.at[j]
        to[:, pl.ds(0, D)] = dot(h1t[...], gp[:, j * D : (j + 1) * D]).astype(bf16)
        to[:, pl.ds(D, hi - lo)] = dot(mt[...], ga[:, lo:hi]).astype(bf16)
        if j == CHUNKS - 1:
            copies[3].wait()
            gh1 = dot_t(gp[...], wp[...])
            xhat1, r1 = norm_parts(tok_ref[...].astype(f32))
            one = jnp.sum(gh1 * xhat1, axis=0, keepdims=True)
            m = gh1 * gain_ref[0:1]
            spread = jnp.mean(m * xhat1, axis=-1, keepdims=True)
            gin_ref[...] = gr[...] + r1 * (m - jnp.mean(m, axis=-1, keepdims=True) - xhat1 * spread)
            row = lax.broadcasted_iota(jnp.int32, (128, D), 0)
            both = jnp.where(row == 0, one, jnp.where(row == 1, second_ref[0:1], 0.0)).astype(bf16)
            to[:, pl.ds(D + 256, 128)] = dot_t(perms[j][...], both).astype(bf16)
        for half, group in enumerate(((sib0, sib1, sib2), (own0, own1, own2))):
            outs.append(
                pltpu.make_async_copy(
                    grads.at[j, pl.ds(half * ROWS, ROWS)], group[j], out_sems.at[2 * j + half]
                )
            )
            outs[-1].start()
    for c in outs:
        c.wait()


def turn_kernel(*refs):
    send, keep, whole = refs[8:]
    at = 0
    for terms in (refs[:4], refs[4:8]):
        total = terms[0][...].astype(f32)
        for t in terms[1:]:
            total = total + t[...].astype(f32)
        whole[:, pl.ds(at, total.shape[1])] = total
        at += total.shape[1]
    send[...] = whole[pl.ds(0, 64), :].astype(bf16)
    keep[...] = whole[pl.ds(64, 64), :].astype(bf16)


def pack_kernel(packed, mixer, expand, reduce, gains, out, wide):
    out[:, pl.ds(0, MIX_AT)] = packed[...]
    out[:, pl.ds(MIX_AT, D)] = mixer[...]
    out[:, pl.ds(GAIN_AT, 128)] = gains[...]
    both = expand[...].astype(f32)
    wide[...] = jnp.zeros(wide.shape, f32)
    wide[0, :, pl.ds(0, FF)] = both[:, :FF]
    wide[1, :, pl.ds(0, FF)] = pltpu.roll(both, FF, 1)[:, :FF]
    wide[2, :, pl.ds(0, FF)] = reduce[...].astype(f32)
    for j in range(CHUNKS):
        for i in range(3):
            out[:, pl.ds(FF_AT + (3 * j + i) * CW, CW)] = wide[i, :, pl.ds(j * CW, CW)].astype(bf16)


def finish_kernel(*refs):
    gots, kepts = refs[:3], refs[3:6]
    packed, mixer, expand, reduce, gain, wide = refs[6:]
    ff = 3 * CW
    for j in range(CHUNKS):
        total = gots[j][...].astype(f32) + kepts[j][...].astype(f32)
        for i in range(3):
            wide[i, :, pl.ds(j * CW, CW)] = total[:, i * CW : (i + 1) * CW]
        packed[:, pl.ds(j * D, D)] = total[:, ff : ff + D]
        lo, hi = MIX_CUTS[j]
        mixer[:, pl.ds(lo, hi - lo)] = total[:, ff + D : ff + D + hi - lo]
    gain[...] = total[:, ff + D + 256 :]
    reduce[...] = wide[2, :, pl.ds(0, FF)]
    lane = lax.broadcasted_iota(jnp.int32, (1, 2 * FF), 1)
    pad = jnp.zeros((8, 2 * FF - CHUNKS * CW), f32)
    gate = jnp.concatenate([wide[0], pad], axis=1)
    up = pltpu.roll(jnp.concatenate([wide[1], pad], axis=1), FF, 1)
    expand[...] = jnp.where(lane < FF, gate, up)


def arr(shape, dtype):
    return jax.ShapeDtypeStruct(shape, dtype)


VSPEC = pl.BlockSpec(memory_space=pltpu.VMEM)
HSPEC = pl.BlockSpec(memory_space=pl.ANY)
DMA = pltpu.SemaphoreType.DMA


def run(
    kernel, name, inputs, out_shape, scratch=(), in_hbm=(), out_hbm=(), after=(), through=(), specs=()
):
    count, outs, extra = len(inputs), len(out_shape), len(after) + len(through)

    def with_order(*refs):
        rest = refs[count + extra :]
        kernel(*refs[:count], *rest[:outs], *rest[outs + len(through) :])

    return pl.pallas_call(
        with_order,
        out_shape=tuple(out_shape) + tuple(arr(t.shape, t.dtype) for t in through),
        grid=(1,) if specs else (),
        in_specs=(list(specs) or [HSPEC if i in in_hbm else VSPEC for i in range(count)])
        + [HSPEC] * extra,
        out_specs=tuple(HSPEC if i in out_hbm else VSPEC for i in range(outs))
        + (HSPEC,) * len(through),
        input_output_aliases={count + len(after) + i: outs + i for i in range(len(through))},
        scratch_shapes=list(scratch),
        compiler_params=pltpu.CompilerParams(vmem_limit_bytes=VMEM),
        cost_estimate=pl.CostEstimate(flops=10**14, bytes_accessed=1024, transcendentals=0),
        name=name,
    )(*inputs, *after, *through)


def token_layout(lengths, slot_count):
    places = jnp.arange(slot_count, dtype=jnp.int32)
    ends = jnp.cumsum(lengths)
    starts = ends - lengths
    segment = jnp.sum((places[:, None] >= ends[None, :]).astype(jnp.int32), axis=1)
    live = places < ends[-1]
    picked = (segment[:, None] == jnp.arange(lengths.shape[0], dtype=jnp.int32)[None, :]).astype(
        jnp.int32
    )
    position = jnp.where(live, places - jnp.sum(picked * starts[None, :], axis=1), 0)
    segment = jnp.where(live, segment, lengths.shape[0] + places)
    return segment, position


def rotary_tables(position):
    frequency = rope_base ** (-(jnp.arange(HD // 2, dtype=f32) * 2.0 / HD))
    angles = position.astype(f32)[:, None] * frequency
    cos, sin = jnp.cos(angles), jnp.sin(angles)
    return (
        jnp.concatenate([cos, cos, cos, cos], axis=-1),
        jnp.concatenate([-sin, sin, -sin, sin], axis=-1),
    )


ORDERS = (("x", "y", "z"), ("y", "z", "x"), ("z", "x", "y"))


def hops(core):
    return (1, 3) if core == 0 else (3, 1)


def row_order(order):
    core = lax.axis_index("c")
    row = jnp.arange(D, dtype=jnp.int32)
    mine, inner = row >= ROWS, row % ROWS
    side = jnp.where(mine, core, 1 - core)
    place = {}
    for axis, size in zip(order, (128, 32, 8)):
        turn = inner // size % 4
        apart = jnp.where(turn == 0, 2, jnp.where(turn == 3, 0, jnp.where((turn == 1) == (side == 0), 1, 3)))
        place[axis] = lax.axis_index(axis) ^ apart
    feature = ((place["y"] * 4 + place["z"]) * 4 + place["x"]) * 16 + side * 8 + inner % 8
    return (feature[:, None] == jnp.arange(D, dtype=jnp.int32)[None, :]).astype(bf16)


def to_partner(a, axis, step):
    pairs = [(i * 2 + c, (i ^ hops(c)[step]) * 2 + c) for i in range(4) for c in range(2)]
    return lax.ppermute(a, (axis, "c"), pairs)


def to_sibling(a):
    return lax.ppermute(a, "c", [(0, 1), (1, 0)])


def added(*arrays):
    return sum(a.astype(f32) for a in arrays).astype(bf16)


class PartSum:
    def __init__(self, order, sib, own):
        self.axis = order[0]
        self.own, self.arrived = own, to_sibling(sib)
        self.lo, self.step, self.got = 0, 0, None

    def piece(self, lo, rows):
        at = slice(lo, lo + rows)
        terms = [self.own[at], self.arrived[at]]
        if self.got is not None:
            terms.append(self.got[lo - self.lo : lo - self.lo + rows])
        return added(*terms)

    def send(self):
        rows = (ROWS - self.lo) // 2
        out = self.piece(self.lo, rows)
        got = to_partner(out, self.axis, self.step)
        self.got = got if self.got is None else (got, self.got)
        self.lo += rows
        self.step += 1
        return out

    def last_terms(self):
        cols = self.own.shape[1]
        got, kept = self.got
        specs = [pl.BlockSpec((128, cols), lambda i, at=at: (at, 0)) for at in (3, 3, 0, 1)]
        return (self.own, self.arrived, got, kept), specs


def halves(a):
    n = a.shape[0] // 2
    return a[:n], a[n:]


def local_step(tokens, cotangent, lengths, weights, perms, part_sum):
    n = tokens.shape[0]
    segment, position = token_layout(lengths, n)
    cos, sin = rotary_tables(position)
    seg_col, seg_row = segment[:, None], segment[None, :]
    tile = arr((n, D), bf16)
    wide = arr((n, D), f32)
    vm = pltpu.VMEM
    gt, *gtts = run(
        cotangent_kernel, "cotangent", (cotangent, seg_col, *perms),
        (tile,) + (arr((D, n), bf16),) * CHUNKS,
    )
    qkv, probs, residual, h1, h2, mixed, gains = run(
        attend_kernel, "attend", (tokens, seg_col, seg_row, cos, sin, weights),
        (arr((n, 3 * D), bf16), arr((H, n, n), f32), wide, tile, tile, tile, arr((8, D), f32)),
        [
            vm((D, 3 * D), bf16), vm((D, D), bf16), vm((D, 128), bf16), vm((n, 3 * D), f32),
            vm((n, n), f32), DMA((3,)),
        ],
        in_hbm=(5,),
    )
    sums, ff, after = (), [], ()
    for j in range(CHUNKS):
        through = (ff[1].own,) if j == 2 else ()
        results = run(
            functools.partial(gated_kernel, j, j > 0), "gated",
            (h2, gt, perms[j], gtts[j], weights, *sums),
            (wide, wide) + (arr((ROWS, 3 * CW), bf16),) * 2,
            [vm((n, D), bf16), vm((n, D), bf16), vm((D, D), bf16), vm((D, n), bf16), vm((D, 3 * CW), bf16)]
            + [vm((n, CW), f32)] * 3
            + [vm((n, CW), bf16)] * 3
            + [vm((D, n), bf16), vm((D, 3 * CW), bf16), DMA((7,)), DMA((6,))],
            in_hbm=(0, 1, 2, 3, 4),
            out_hbm=(2, 3),
            after=after,
            through=through,
        )
        sums = results[:2]
        ff.append(part_sum(ORDERS[j], results[2], results[3]))
        if j == 2:
            ff[1].own = results[4]
        if j > 0:
            after = (ff[j - 1].send(),)
    branch, gh2 = sums
    block_output, gr, ga, second, gp = run(
        heads_kernel, "heads",
        (gt, seg_col, gains, residual, branch, gh2, cos, sin, qkv, probs, weights),
        (tile, wide, tile, arr((8, D), f32), arr((n, 3 * D), bf16)),
        [vm((D, D), bf16), vm((n, 3 * D), bf16), vm((H, n, n), f32), vm((n, D), bf16), DMA((3,))],
        in_hbm=(8, 9, 10),
        after=after,
    )
    after = (ff[2].send(), ff[0].send())
    input_grad, *pieces = run(
        back_kernel, "back", (h1, mixed, ga, gp, tokens, gr, gains, second, *perms, weights),
        (wide,) + (arr((ROWS, A_COLS), bf16),) * 6,
        [vm((D, D), bf16)] * 3
        + [vm((D, 3 * D), bf16), vm((D, n), bf16), vm((D, n), bf16), vm((3, D, A_COLS), bf16)]
        + [DMA((4,)), DMA((6,))],
        in_hbm=(8, 9, 10, 11),
        out_hbm=(1, 2, 3, 4, 5, 6),
        after=after,
        through=(ff[0].own, ff[1].own),
    )
    ff[0].own, ff[1].own = pieces[6:]
    att = [part_sum(ORDERS[j], pieces[j], pieces[3 + j]) for j in range(CHUNKS)]
    return block_output, input_grad, ff, att


def summed(ff, att):
    for part in (ff[1], att[0], ff[2], att[1], att[2], *att):
        part.send()
    pairs = []
    for f, a in zip(ff, att):
        (f_terms, f_specs), (a_terms, a_specs) = f.last_terms(), a.last_terms()
        cols = f.own.shape[1] + a.own.shape[1]
        pairs.append(
            run(
                turn_kernel, "turn", f_terms + a_terms, (arr((64, cols), bf16),) * 2,
                [pltpu.VMEM((128, cols), f32)], specs=f_specs + a_specs,
            )
        )
    for ring, step in ((1, 0), (1, 1), (2, 0), (2, 1)):
        gots = [to_partner(p[0], order[ring], step) for p, order in zip(pairs, ORDERS)]
        kept = [p[1] for p in pairs]
        if (ring, step) != (2, 1):
            pairs = [halves(added(g, k)) for g, k in zip(gots, kept)]
    return gots, kept


def own_rows(gots, kept):
    n = 8
    *grads, gains = run(
        finish_kernel, "finish", (*gots, *kept),
        tuple(arr((n, c), f32) for c in (3 * D, D, 2 * FF, FF, 128)),
        [pltpu.VMEM((3, n, CHUNKS * CW), f32)],
    )
    return (*grads, gains[:, 0], gains[:, 1])


def body(
    tokens, packed_proj, mixer_proj, expand_proj, reduce_proj, first_gain, second_gain,
    sequence_lengths, cotangent,
):
    gains = jnp.pad(jnp.stack([first_gain, second_gain], axis=1), ((0, 0), (0, 126)))
    (shard,) = run(
        pack_kernel, "pack", (packed_proj, mixer_proj, expand_proj, reduce_proj, gains),
        (arr((8, W_COLS), bf16),), [pltpu.VMEM((3, 8, CHUNKS * CW), f32)],
    )
    weights = lax.all_gather(shard, ALL, axis=0, tiled=True)
    perms = [row_order(order) for order in ORDERS]
    block_output, input_grad, ff, att = local_step(
        tokens, cotangent, sequence_lengths, weights, perms, PartSum
    )
    return (block_output, input_grad, *own_rows(*summed(ff, att)))


def solution(mesh):
    torus = Mesh(mesh.devices.reshape(4, 4, 4, 2), ALL)
    row, flat = P(ALL, None), P(ALL)
    return jax.shard_map(
        body,
        mesh=torus,
        in_specs=(row,) * 5 + (flat, flat, flat, row),
        out_specs=(row,) * 6 + (flat, flat),
        check_vma=False,
    )
```

```python
import functools

import jax
import jax.numpy as jnp
from jax import lax
from jax.experimental import pallas as pl
from jax.experimental.pallas import tpu as pltpu
from jax.sharding import Mesh
from jax.sharding import PartitionSpec as P

H = 16
HD = 64
PAIR = 2 * HD
PAIRS = H // 2
epsilon = 1e-05
rope_base = 160000.0
masked_score = -1e30
AXES = ("y", "z", "x")
ALL = ("y", "z", "x", "c")
VMEM = 60 * 1024 * 1024
bf16 = jnp.bfloat16
f32 = jnp.float32

D = 1024
FF = 2624
CHUNKS = 3
CW = 896
MIX_AT = 3 * D
GAIN_AT = 4 * D
FF_AT = 4 * D + 128
W_COLS = FF_AT + CHUNKS * 3 * CW
ROWS = 512
MIX_CUTS = ((0, 384), (384, 768), (768, 1024))
A_COLS = D + 384


def dot(a, b):
    return lax.dot_general(a, b, (((1,), (0,)), ((), ())), preferred_element_type=f32)


def dot_t(a, b):
    return lax.dot_general(a, b, (((1,), (1,)), ((), ())), preferred_element_type=f32)


def dot_first(a, b):
    return lax.dot_general(a, b, (((0,), (0,)), ((), ())), preferred_element_type=f32)


def norm_parts(values):
    centered = values - jnp.mean(values, axis=-1, keepdims=True)
    scale = lax.rsqrt(jnp.mean(centered * centered, axis=-1, keepdims=True) + epsilon)
    return centered * scale, scale


def half_swapped(v, low_half):
    return jnp.where(low_half, pltpu.roll(v, PAIR - HD // 2, 1), pltpu.roll(v, HD // 2, 1))


def pair_slice(p, at=0):
    return pl.ds(pl.multiple_of(p * PAIR + at, PAIR), PAIR)


def cotangent_kernel(cot_ref, seg_ref, *refs):
    perms, gt_ref, gtts = refs[:CHUNKS], refs[CHUNKS], refs[CHUNKS + 1 :]
    gt = jnp.where(seg_ref[...] < 4, cot_ref[...].astype(f32), 0.0).astype(bf16)
    gt_ref[...] = gt
    for perm, gtt in zip(perms, gtts):
        gtt[...] = dot_t(perm[...], gt).astype(bf16)


def attend_kernel(
    tok_ref, seg_ref, segt_ref, cos_ref, sin_ref, w_ref,
    qkv_hbm, prob_hbm, res_ref, h1_ref, h2_ref, mixed, gain_ref,
    wp, wm, wg, packed, bias, qkv, prob, sems, out_sems,
):
    copies = [
        pltpu.make_async_copy(w_ref.at[:, pl.ds(GAIN_AT, 128)], wg, sems.at[0]),
        pltpu.make_async_copy(w_ref.at[:, pl.ds(0, 3 * D)], wp, sems.at[1]),
        pltpu.make_async_copy(w_ref.at[:, pl.ds(MIX_AT, D)], wm, sems.at[2]),
    ]
    for c in copies:
        c.start()
    tokens = tok_ref[...].astype(f32)
    xhat, _ = norm_parts(tokens)
    bias[...] = jnp.where(seg_ref[...] == segt_ref[...], 0.0, masked_score)
    copies[0].wait()
    gains = jnp.transpose(wg[...].astype(f32))[:8]
    gain_ref[...] = gains
    h1 = (xhat * gains[0:1]).astype(bf16)
    h1_ref[...] = h1
    copies[1].wait()
    packed[...] = dot(h1, wp[...])
    low_half = lax.broadcasted_iota(jnp.int32, (1, PAIR), 1) % HD < HD // 2
    first = lax.broadcasted_iota(jnp.int32, (1, PAIR), 1) < HD
    zero = jnp.zeros((), bf16)

    def pair(p, carry):
        cos, sin = cos_ref[...], sin_ref[...]
        q = packed[:, pair_slice(p)]
        k = packed[:, pair_slice(p, D)]
        q = (q * cos + half_swapped(q, low_half) * sin).astype(bf16)
        k = (k * cos + half_swapped(k, low_half) * sin).astype(bf16)
        v = packed[:, pair_slice(p, 2 * D)].astype(bf16)
        qkv[:, pair_slice(p)] = q
        qkv[:, pair_slice(p, D)] = k
        qkv[:, pair_slice(p, 2 * D)] = v
        outs = []
        for side in range(2):
            mine = first if side == 0 else jnp.logical_not(first)
            scores = dot_t(jnp.where(mine, q, zero), k) * (HD**-0.5) + bias[...]
            top = jnp.max(scores, axis=-1, keepdims=True)
            e = jnp.exp(scores - top)
            probs = e * (1.0 / jnp.sum(e, axis=-1, keepdims=True))
            prob[2 * p + side] = probs
            outs.append(dot(probs.astype(bf16), v))
        mixed[:, pair_slice(p)] = jnp.where(first, outs[0], outs[1]).astype(bf16)
        return carry

    outs = []
    for i in range(2):
        lax.fori_loop(i * PAIRS // 2, (i + 1) * PAIRS // 2, pair, 0)
        part = pl.ds(i * PAIRS, PAIRS)
        outs.append(pltpu.make_async_copy(prob.at[part], prob_hbm.at[part], out_sems.at[i]))
        outs[-1].start()
    outs.append(pltpu.make_async_copy(qkv, qkv_hbm, out_sems.at[2]))
    outs[-1].start()
    copies[2].wait()
    residual = tokens + dot(mixed[...], wm[...])
    res_ref[...] = residual
    xhat2, _ = norm_parts(residual)
    h2_ref[...] = (xhat2 * gains[1:2]).astype(bf16)
    for c in outs:
        c.wait()


def started(pairs, sems):
    copies = [pltpu.make_async_copy(a, b, sems.at[i]) for i, (a, b) in enumerate(pairs)]
    for c in copies:
        c.start()
    return copies


def gated_kernel(chunk, has_sum, h2_hbm, gt_hbm, perm_hbm, gtt_hbm, w_hbm, *refs):
    if has_sum:
        branch_in, gh2_in = refs[:2]
        refs = refs[2:]
    branch_hbm, gh2_hbm, sib_hbm, own_hbm = refs[:4]
    h2, gt, perm, gtt, w, gate, up, gh, hid, gg, gu, h2t, grads, totals, sems, out_sems = refs[4:]
    base = FF_AT + chunk * 3 * CW
    pieces = [
        (w_hbm.at[:, pl.ds(base + i * CW, CW)], w.at[:, pl.ds(i * CW, CW)]) for i in range(3)
    ]
    copies = started(
        [(h2_hbm, h2), pieces[0], pieces[1], (gt_hbm, gt), pieces[2], (perm_hbm, perm), (gtt_hbm, gtt)],
        sems,
    )
    sums_in = []
    if has_sum:
        sums_in = [
            pltpu.make_async_copy(a, totals.at[i], out_sems.at[i])
            for i, a in enumerate((branch_in, gh2_in))
        ]
        for c in sums_in:
            c.start()
    copies[0].wait()
    copies[1].wait()
    gate[...] = dot(h2[...], w[:, :CW])
    copies[2].wait()
    up[...] = dot(h2[...], w[:, CW : 2 * CW])
    copies[3].wait()
    copies[4].wait()
    gh[...] = dot(gt[...], w[:, 2 * CW :])
    copies[5].wait()
    h2t[...] = dot_t(perm[...], h2[...]).astype(bf16)
    size = 16

    def rows(i, carry):
        r = pl.ds(pl.multiple_of(i * size, size), size)
        g, u, d = gate[r, :], up[r, :], gh[r, :]
        cdf = 0.5 * (1.0 + lax.erf(g * (0.5**0.5)))
        act = g * cdf
        slope = cdf + g * (jnp.exp(-0.5 * g * g) * 0.3989422804014327)
        hid[r, :] = (act * u).astype(bf16)
        gg[r, :] = (d * u * slope).astype(bf16)
        gu[r, :] = (d * act).astype(bf16)
        return carry

    lax.fori_loop(0, gate.shape[0] // size, rows, 0)
    branch = dot_t(hid[...], w[:, 2 * CW :])
    gh2 = dot_t(gg[...], w[:, :CW]) + dot_t(gu[...], w[:, CW : 2 * CW])
    for c in sums_in:
        c.wait()
    totals[0] = branch + totals[0] if has_sum else branch
    totals[1] = gh2 + totals[1] if has_sum else gh2
    outs = [
        pltpu.make_async_copy(totals.at[i], to, out_sems.at[i])
        for i, to in enumerate((branch_hbm, gh2_hbm))
    ]
    for c in outs:
        c.start()
    copies[6].wait()
    for half, to in enumerate((sib_hbm, own_hbm)):
        rows_at = pl.ds(half * ROWS, ROWS)
        for i, (left, right) in enumerate(((h2t, gg), (h2t, gu), (gtt, hid))):
            cols = pl.ds(i * CW, CW)
            grads[rows_at, cols] = dot(left[rows_at, :], right[...]).astype(bf16)
            outs.append(
                pltpu.make_async_copy(
                    grads.at[rows_at, cols], to.at[:, cols], out_sems.at[2 + 3 * half + i]
                )
            )
            outs[-1].start()
    for c in outs:
        c.wait()


def back_kernel(
    gain_ref, seg_ref, cos_ref, sin_ref, gt_ref, res_hbm, branch_hbm, gh2_hbm, qkv_hbm, prob_hbm,
    h1_hbm, mixed_hbm, tok_hbm, perm0, perm1, perm2, w_hbm,
    out_ref, gin_ref, sib0, sib1, sib2, own0, own1, own2,
    res_ref, branch_ref, gh2_ref, qkv, prob, h1, mixed, tok, p0, p1, p2, wp, wm,
    gr, ga_ref, gm, gp, h1t, mt, grads, sems, out_sems,
):
    perms = (p0, p1, p2)
    copies = started(
        [
            (res_hbm, res_ref), (branch_hbm, branch_ref), (gh2_hbm, gh2_ref),
            (w_hbm.at[:, pl.ds(MIX_AT, D)], wm), (qkv_hbm, qkv), (prob_hbm, prob),
            (h1_hbm, h1), (mixed_hbm, mixed), (perm0, p0), (perm1, p1), (perm2, p2),
            (w_hbm.at[:, pl.ds(0, 3 * D)], wp), (tok_hbm, tok),
        ],
        sems,
    )
    for c in copies[:3]:
        c.wait()
    residual = res_ref[...]
    live = seg_ref[...] < 4
    out_ref[...] = jnp.where(live, residual + branch_ref[...], 0.0).astype(bf16)
    xhat2, r2 = norm_parts(residual)
    gh2 = gh2_ref[...]
    second = jnp.sum(gh2 * xhat2, axis=0, keepdims=True)
    n = gh2 * gain_ref[1:2]
    spread = jnp.mean(n * xhat2, axis=-1, keepdims=True)
    grad_res = gt_ref[...].astype(f32) + r2 * (
        n - jnp.mean(n, axis=-1, keepdims=True) - xhat2 * spread
    )
    gr[...] = grad_res
    ga = grad_res.astype(bf16)
    ga_ref[...] = ga
    copies[3].wait()
    gm[...] = dot_t(ga, wm[...]).astype(bf16)
    copies[4].wait()
    copies[5].wait()
    low_half = lax.broadcasted_iota(jnp.int32, (1, PAIR), 1) % HD < HD // 2
    first = lax.broadcasted_iota(jnp.int32, (1, PAIR), 1) < HD
    zero = jnp.zeros((), bf16)

    def pair(p, carry):
        cos, sin = cos_ref[...], sin_ref[...]
        q = qkv[:, pair_slice(p)]
        k = qkv[:, pair_slice(p, D)]
        v = qkv[:, pair_slice(p, 2 * D)]
        g = gm[:, pair_slice(p)]
        dq, dk, dv = [], [], []
        for side in range(2):
            mine = first if side == 0 else jnp.logical_not(first)
            probs = prob[2 * p + side]
            grad_probs = dot_t(jnp.where(mine, g, zero), v)
            weighted = probs * grad_probs
            delta = jnp.sum(weighted, axis=-1, keepdims=True)
            gs = (weighted - probs * delta).astype(bf16)
            dq.append(dot(gs, k))
            dk.append(dot_first(gs, q))
            dv.append(dot_first(probs.astype(bf16), g))
        dq = jnp.where(first, dq[0], dq[1]) * (HD**-0.5)
        dk = jnp.where(first, dk[0], dk[1]) * (HD**-0.5)
        dv = jnp.where(first, dv[0], dv[1])
        gp[:, pair_slice(p)] = (dq * cos - half_swapped(dq, low_half) * sin).astype(bf16)
        gp[:, pair_slice(p, D)] = (dk * cos - half_swapped(dk, low_half) * sin).astype(bf16)
        gp[:, pair_slice(p, 2 * D)] = dv.astype(bf16)
        return carry

    lax.fori_loop(0, PAIRS, pair, 0)
    copies[6].wait()
    copies[7].wait()
    outs = []
    for j in range(CHUNKS):
        copies[8 + j].wait()
        h1t[...] = dot_t(perms[j][...], h1[...]).astype(bf16)
        mt[...] = dot_t(perms[j][...], mixed[...]).astype(bf16)
        lo, hi = MIX_CUTS[j]
        to = grads.at[j]
        to[:, pl.ds(0, D)] = dot(h1t[...], gp[:, j * D : (j + 1) * D]).astype(bf16)
        to[:, pl.ds(D, hi - lo)] = dot(mt[...], ga_ref[:, lo:hi]).astype(bf16)
        if j == CHUNKS - 1:
            copies[11].wait()
            copies[12].wait()
            gh1 = dot_t(gp[...], wp[...])
            xhat1, r1 = norm_parts(tok[...].astype(f32))
            one = jnp.sum(gh1 * xhat1, axis=0, keepdims=True)
            m = gh1 * gain_ref[0:1]
            spread = jnp.mean(m * xhat1, axis=-1, keepdims=True)
            gin_ref[...] = gr[...] + r1 * (m - jnp.mean(m, axis=-1, keepdims=True) - xhat1 * spread)
            row = lax.broadcasted_iota(jnp.int32, (128, D), 0)
            both = jnp.where(row == 0, one, jnp.where(row == 1, second, 0.0)).astype(bf16)
            to[:, pl.ds(D + 256, 128)] = dot_t(perms[j][...], both).astype(bf16)
        for half, group in enumerate(((sib0, sib1, sib2), (own0, own1, own2))):
            outs.append(
                pltpu.make_async_copy(
                    grads.at[j, pl.ds(half * ROWS, ROWS)], group[j], out_sems.at[2 * j + half]
                )
            )
            outs[-1].start()
    for c in outs:
        c.wait()


def turn_kernel(ff_terms, *refs):
    send, keep, whole = refs[ff_terms + 4 :]
    at = 0
    for terms in (refs[:ff_terms], refs[ff_terms : ff_terms + 4]):
        total = terms[0][...].astype(f32)
        for t in terms[1:]:
            total = total + t[...].astype(f32)
        whole[:, pl.ds(at, total.shape[1])] = total
        at += total.shape[1]
    send[...] = whole[pl.ds(0, 64), :].astype(bf16)
    keep[...] = whole[pl.ds(64, 64), :].astype(bf16)


def pack_kernel(packed, mixer, expand, reduce, gains, out, wide):
    out[:, pl.ds(0, MIX_AT)] = packed[...]
    out[:, pl.ds(MIX_AT, D)] = mixer[...]
    out[:, pl.ds(GAIN_AT, 128)] = gains[...]
    both = expand[...].astype(f32)
    wide[...] = jnp.zeros(wide.shape, f32)
    wide[0, :, pl.ds(0, FF)] = both[:, :FF]
    wide[1, :, pl.ds(0, FF)] = pltpu.roll(both, FF, 1)[:, :FF]
    wide[2, :, pl.ds(0, FF)] = reduce[...].astype(f32)
    for j in range(CHUNKS):
        for i in range(3):
            out[:, pl.ds(FF_AT + (3 * j + i) * CW, CW)] = wide[i, :, pl.ds(j * CW, CW)].astype(bf16)


def finish_kernel(*refs):
    gots, kepts = refs[:3], refs[3:6]
    packed, mixer, expand, reduce, gain, wide = refs[6:]
    ff = 3 * CW
    for j in range(CHUNKS):
        total = gots[j][...].astype(f32) + kepts[j][...].astype(f32)
        for i in range(3):
            wide[i, :, pl.ds(j * CW, CW)] = total[:, i * CW : (i + 1) * CW]
        packed[:, pl.ds(j * D, D)] = total[:, ff : ff + D]
        lo, hi = MIX_CUTS[j]
        mixer[:, pl.ds(lo, hi - lo)] = total[:, ff + D : ff + D + hi - lo]
    gain[...] = jnp.transpose(total[:, ff + D + 256 :])[:8]
    reduce[...] = wide[2, :, pl.ds(0, FF)]
    lane = lax.broadcasted_iota(jnp.int32, (1, 2 * FF), 1)
    pad = jnp.zeros((8, 2 * FF - CHUNKS * CW), f32)
    gate = jnp.concatenate([wide[0], pad], axis=1)
    up = pltpu.roll(jnp.concatenate([wide[1], pad], axis=1), FF, 1)
    expand[...] = jnp.where(lane < FF, gate, up)


def arr(shape, dtype):
    return jax.ShapeDtypeStruct(shape, dtype)


VSPEC = pl.BlockSpec(memory_space=pltpu.VMEM)
HSPEC = pl.BlockSpec(memory_space=pl.ANY)
DMA = pltpu.SemaphoreType.DMA


def run(
    kernel, name, inputs, out_shape, scratch=(), in_hbm=(), out_hbm=(), after=(), through=(), specs=()
):
    count, outs, extra = len(inputs), len(out_shape), len(after) + len(through)

    def with_order(*refs):
        rest = refs[count + extra :]
        kernel(*refs[:count], *rest[:outs], *rest[outs + len(through) :])

    return pl.pallas_call(
        with_order,
        out_shape=tuple(out_shape) + tuple(arr(t.shape, t.dtype) for t in through),
        grid=(1,) if specs else (),
        in_specs=(list(specs) or [HSPEC if i in in_hbm else VSPEC for i in range(count)])
        + [HSPEC] * extra,
        out_specs=tuple(HSPEC if i in out_hbm else VSPEC for i in range(outs))
        + (HSPEC,) * len(through),
        input_output_aliases={count + len(after) + i: outs + i for i in range(len(through))},
        scratch_shapes=list(scratch),
        compiler_params=pltpu.CompilerParams(vmem_limit_bytes=VMEM),
        cost_estimate=pl.CostEstimate(flops=10**14, bytes_accessed=1024, transcendentals=0),
        name=name,
    )(*inputs, *after, *through)


def token_layout(lengths, slot_count):
    places = jnp.arange(slot_count, dtype=jnp.int32)
    ends = jnp.cumsum(lengths)
    starts = ends - lengths
    segment = jnp.sum((places[:, None] >= ends[None, :]).astype(jnp.int32), axis=1)
    live = places < ends[-1]
    picked = (segment[:, None] == jnp.arange(lengths.shape[0], dtype=jnp.int32)[None, :]).astype(
        jnp.int32
    )
    position = jnp.where(live, places - jnp.sum(picked * starts[None, :], axis=1), 0)
    segment = jnp.where(live, segment, lengths.shape[0] + places)
    return segment, position


def rotary_tables(position):
    frequency = rope_base ** (-(jnp.arange(HD // 2, dtype=f32) * 2.0 / HD))
    angles = position.astype(f32)[:, None] * frequency
    cos, sin = jnp.cos(angles), jnp.sin(angles)
    return (
        jnp.concatenate([cos, cos, cos, cos], axis=-1),
        jnp.concatenate([-sin, sin, -sin, sin], axis=-1),
    )


ORDERS = (("x", "y", "z"), ("y", "z", "x"), ("z", "x", "y"))


def hops(core):
    return (1, 3) if core == 0 else (3, 1)


def row_order(order):
    core = lax.axis_index("c")
    row = jnp.arange(D, dtype=jnp.int32)
    mine, inner = row >= ROWS, row % ROWS
    side = jnp.where(mine, core, 1 - core)
    place = {}
    for axis, size in zip(order, (128, 32, 8)):
        turn = inner // size % 4
        apart = jnp.where(turn == 0, 2, jnp.where(turn == 3, 0, jnp.where((turn == 1) == (side == 0), 1, 3)))
        place[axis] = lax.axis_index(axis) ^ apart
    feature = ((place["y"] * 4 + place["z"]) * 4 + place["x"]) * 16 + side * 8 + inner % 8
    return (feature[:, None] == jnp.arange(D, dtype=jnp.int32)[None, :]).astype(bf16)


def to_partner(a, axis, step):
    pairs = [(i * 2 + c, (i ^ hops(c)[step]) * 2 + c) for i in range(4) for c in range(2)]
    return lax.ppermute(a, (axis, "c"), pairs)


def to_sibling(a):
    return lax.ppermute(a, "c", [(0, 1), (1, 0)])


def added(*arrays):
    total = arrays[0]
    for a in arrays[1:]:
        total = total + a
    return total


class PartSum:
    def __init__(self, order, sib, own):
        self.axis = order[0]
        self.own, self.arrived = own, to_sibling(sib)
        self.lo, self.step, self.got = 0, 0, None

    def piece(self, lo, rows):
        at = slice(lo, lo + rows)
        terms = [self.own[at], self.arrived[at]]
        if self.got is not None:
            terms.append(self.got[lo - self.lo : lo - self.lo + rows])
        return added(*terms)

    def send(self):
        rows = (ROWS - self.lo) // 2
        out = self.piece(self.lo, rows)
        got = to_partner(out, self.axis, self.step)
        self.got = got if self.got is None else (got, self.got)
        self.lo += rows
        self.step += 1
        return out

    def last_terms(self):
        cols = self.own.shape[1]
        got, kept = self.got
        specs = [pl.BlockSpec((128, cols), lambda i, at=at: (at, 0)) for at in (3, 3, 0, 1)]
        return (self.own, self.arrived, got, kept), specs

    def total(self):
        got, kept = self.got
        at = slice(self.lo, ROWS)
        return (added(self.own[at], self.arrived[at], got, kept[ROWS // 4 :]),), [VSPEC]


def halves(a):
    n = a.shape[0] // 2
    return a[:n], a[n:]


def local_step(tokens, cotangent, lengths, weights, perms, part_sum):
    n = tokens.shape[0]
    segment, position = token_layout(lengths, n)
    cos, sin = rotary_tables(position)
    seg_col, seg_row = segment[:, None], segment[None, :]
    tile = arr((n, D), bf16)
    wide = arr((n, D), f32)
    vm = pltpu.VMEM
    gt, *gtts = run(
        cotangent_kernel, "cotangent", (cotangent, seg_col, *perms),
        (tile,) + (arr((D, n), bf16),) * CHUNKS,
    )
    qkv, probs, residual, h1, h2, mixed, gains = run(
        attend_kernel, "attend", (tokens, seg_col, seg_row, cos, sin, weights),
        (arr((n, 3 * D), bf16), arr((H, n, n), f32), wide, tile, tile, tile, arr((8, D), f32)),
        [
            vm((D, 3 * D), bf16), vm((D, D), bf16), vm((D, 128), bf16), vm((n, 3 * D), f32),
            vm((n, n), f32), vm((n, 3 * D), bf16), vm((H, n, n), f32), DMA((3,)), DMA((3,)),
        ],
        in_hbm=(5,),
        out_hbm=(0, 1),
    )
    sums, ff, after = (), [], ()
    for j in range(CHUNKS):
        through = (ff[1].own,) if j == 2 else ()
        results = run(
            functools.partial(gated_kernel, j, j > 0), "gated",
            (h2, gt, perms[j], gtts[j], weights, *sums),
            (wide, wide) + (arr((ROWS, 3 * CW), bf16),) * 2,
            [vm((n, D), bf16), vm((n, D), bf16), vm((D, D), bf16), vm((D, n), bf16), vm((D, 3 * CW), bf16)]
            + [vm((n, CW), f32)] * 3
            + [vm((n, CW), bf16)] * 3
            + [vm((D, n), bf16), vm((D, 3 * CW), bf16), vm((2, n, D), f32), DMA((7,)), DMA((8,))],
            in_hbm=range(5 + len(sums)),
            out_hbm=range(4),
            after=after,
            through=through,
        )
        sums = results[:2]
        ff.append(part_sum(ORDERS[j], results[2], results[3]))
        if j == 2:
            ff[1].own = results[4]
        if j > 0:
            after = (ff[j - 1].send(),)
    branch, gh2 = sums
    after += (ff[2].send(),)
    block_output, input_grad, *pieces = run(
        back_kernel, "back",
        (gains, seg_col, cos, sin, gt, residual, branch, gh2, qkv, probs, h1, mixed, tokens, *perms, weights),
        (tile, wide) + (arr((ROWS, A_COLS), bf16),) * 6,
        [vm((n, D), f32)] * 3
        + [vm((n, 3 * D), bf16), vm((H, n, n), f32)]
        + [vm((n, D), bf16)] * 3
        + [vm((D, D), bf16)] * 3
        + [vm((D, 3 * D), bf16), vm((D, D), bf16), vm((n, D), f32), vm((n, D), bf16), vm((n, D), bf16)]
        + [vm((n, 3 * D), bf16), vm((D, n), bf16), vm((D, n), bf16), vm((3, D, A_COLS), bf16)]
        + [DMA((13,)), DMA((6,))],
        in_hbm=range(5, 17),
        out_hbm=range(2, 8),
        after=after,
        through=(ff[0].own, ff[1].own),
    )
    ff[0].own, ff[1].own = pieces[6:]
    att = [part_sum(ORDERS[j], pieces[j], pieces[3 + j]) for j in range(CHUNKS)]
    return block_output, input_grad, ff, att


def summed(ff, att):
    for f in ff:
        f.send()
    for f, a in zip(ff, att):
        f.own, _ = lax.optimization_barrier((f.own, a.send()))
    for a in att:
        a.send()
    pairs = []
    for f, a in zip(ff, att):
        f_terms, f_specs = f.total()
        a_terms, a_specs = a.last_terms()
        cols = f.own.shape[1] + a.own.shape[1]
        pairs.append(
            run(
                functools.partial(turn_kernel, len(f_terms)), "turn", f_terms + a_terms, (arr((64, cols), bf16),) * 2,
                [pltpu.VMEM((128, cols), f32)], specs=f_specs + a_specs,
            )
        )
    for ring, step in ((1, 0), (1, 1), (2, 0), (2, 1)):
        gots = [to_partner(p[0], order[ring], step) for p, order in zip(pairs, ORDERS)]
        kept = [p[1] for p in pairs]
        if (ring, step) != (2, 1):
            pairs = [halves(added(g, k)) for g, k in zip(gots, kept)]
    return gots, kept


def own_rows(gots, kept):
    n = 8
    *grads, gains = run(
        finish_kernel, "finish", (*gots, *kept),
        tuple(arr((n, c), f32) for c in (3 * D, D, 2 * FF, FF, 8)),
        [pltpu.VMEM((3, n, CHUNKS * CW), f32)],
    )
    return (*grads, gains[0], gains[1])


def body(
    tokens, packed_proj, mixer_proj, expand_proj, reduce_proj, first_gain, second_gain,
    sequence_lengths, cotangent,
):
    gains = jnp.pad(jnp.stack([first_gain, second_gain], axis=1), ((0, 0), (0, 126)))
    (shard,) = run(
        pack_kernel, "pack", (packed_proj, mixer_proj, expand_proj, reduce_proj, gains),
        (arr((8, W_COLS), bf16),), [pltpu.VMEM((3, 8, CHUNKS * CW), f32)],
    )
    weights = lax.all_gather(shard, ALL, axis=0, tiled=True)
    perms = [row_order(order) for order in ORDERS]
    block_output, input_grad, ff, att = local_step(
        tokens, cotangent, sequence_lengths, weights, perms, PartSum
    )
    return (block_output, input_grad, *own_rows(*summed(ff, att)))


def solution(mesh):
    torus = Mesh(mesh.devices.reshape(4, 4, 4, 2), ALL)
    row, flat = P(ALL, None), P(ALL)
    return jax.shard_map(
        body,
        mesh=torus,
        in_specs=(row,) * 5 + (flat, flat, flat, row),
        out_specs=(row,) * 6 + (flat, flat),
        check_vma=False,
    )
```

```python
import functools

import jax
import jax.numpy as jnp
from jax import lax
from jax.experimental import pallas as pl
from jax.experimental.pallas import tpu as pltpu
from jax.sharding import Mesh
from jax.sharding import PartitionSpec as P

H = 16
HD = 64
PAIR = 2 * HD
PAIRS = H // 2
epsilon = 1e-05
rope_base = 160000.0
masked_score = -1e30
AXES = ("y", "z", "x")
ALL = ("y", "z", "x", "c")
VMEM = 60 * 1024 * 1024
bf16 = jnp.bfloat16
f32 = jnp.float32

D = 1024
FF = 2624
CHUNKS = 3
CW = 896
MIX_AT = 3 * D
GAIN_AT = 4 * D
FF_AT = 4 * D + 128
W_COLS = FF_AT + CHUNKS * 3 * CW
ROWS = 512
MIX_CUTS = ((0, 384), (384, 768), (768, 1024))
A_COLS = D + 384


def dot(a, b):
    return lax.dot_general(a, b, (((1,), (0,)), ((), ())), preferred_element_type=f32)


def dot_t(a, b):
    return lax.dot_general(a, b, (((1,), (1,)), ((), ())), preferred_element_type=f32)


def dot_first(a, b):
    return lax.dot_general(a, b, (((0,), (0,)), ((), ())), preferred_element_type=f32)


def norm_parts(values):
    centered = values - jnp.mean(values, axis=-1, keepdims=True)
    scale = lax.rsqrt(jnp.mean(centered * centered, axis=-1, keepdims=True) + epsilon)
    return centered * scale, scale


def half_swapped(v, low_half):
    return jnp.where(low_half, pltpu.roll(v, PAIR - HD // 2, 1), pltpu.roll(v, HD // 2, 1))


def pair_slice(p, at=0):
    return pl.ds(p * PAIR + at, PAIR)


def cotangent_kernel(cot_ref, seg_ref, *refs):
    perms, gt_ref, gtts = refs[:CHUNKS], refs[CHUNKS], refs[CHUNKS + 1 :]
    gt = jnp.where(seg_ref[...] < 4, cot_ref[...].astype(f32), 0.0).astype(bf16)
    gt_ref[...] = gt
    for perm, gtt in zip(perms, gtts):
        gtt[...] = dot_t(perm[...], gt).astype(bf16)


def attend_kernel(
    tok_ref, seg_ref, segt_ref, cos_ref, sin_ref, w_ref,
    qkv_hbm, prob_hbm, res_ref, h1_ref, h2_ref, mixed, gain_ref,
    wp, wm, wg, packed, bias, qkv, prob, sems, out_sems,
):
    copies = [
        pltpu.make_async_copy(w_ref.at[:, pl.ds(GAIN_AT, 128)], wg, sems.at[0]),
        pltpu.make_async_copy(w_ref.at[:, pl.ds(0, 3 * D)], wp, sems.at[1]),
        pltpu.make_async_copy(w_ref.at[:, pl.ds(MIX_AT, D)], wm, sems.at[2]),
    ]
    for c in copies:
        c.start()
    tokens = tok_ref[...].astype(f32)
    xhat, _ = norm_parts(tokens)
    bias[...] = jnp.where(seg_ref[...] == segt_ref[...], 0.0, masked_score)
    copies[0].wait()
    gains = jnp.transpose(wg[...].astype(f32))[:8]
    gain_ref[...] = gains
    h1 = (xhat * gains[0:1]).astype(bf16)
    h1_ref[...] = h1
    copies[1].wait()
    packed[...] = dot(h1, wp[...])
    low_half = lax.broadcasted_iota(jnp.int32, (1, PAIR), 1) % HD < HD // 2
    first = lax.broadcasted_iota(jnp.int32, (1, PAIR), 1) < HD
    zero = jnp.zeros((), bf16)

    def pair(p):
        cos, sin = cos_ref[...], sin_ref[...]
        q = packed[:, pair_slice(p)]
        k = packed[:, pair_slice(p, D)]
        q = (q * cos + half_swapped(q, low_half) * sin).astype(bf16)
        k = (k * cos + half_swapped(k, low_half) * sin).astype(bf16)
        v = packed[:, pair_slice(p, 2 * D)].astype(bf16)
        qkv[:, pair_slice(p)] = q
        qkv[:, pair_slice(p, D)] = k
        qkv[:, pair_slice(p, 2 * D)] = v
        outs = []
        for side in range(2):
            mine = first if side == 0 else jnp.logical_not(first)
            scores = dot_t(jnp.where(mine, q, zero), k) * (HD**-0.5) + bias[...]
            top = jnp.max(scores, axis=-1, keepdims=True)
            e = jnp.exp(scores - top)
            probs = e * (1.0 / jnp.sum(e, axis=-1, keepdims=True))
            prob[2 * p + side] = probs
            outs.append(dot(probs.astype(bf16), v))
        mixed[:, pair_slice(p)] = jnp.where(first, outs[0], outs[1]).astype(bf16)

    outs = []
    for i in range(2):
        for p in range(i * PAIRS // 2, (i + 1) * PAIRS // 2):
            pair(p)
        part = pl.ds(i * PAIRS, PAIRS)
        outs.append(pltpu.make_async_copy(prob.at[part], prob_hbm.at[part], out_sems.at[i]))
        outs[-1].start()
    outs.append(pltpu.make_async_copy(qkv, qkv_hbm, out_sems.at[2]))
    outs[-1].start()
    copies[2].wait()
    residual = tokens + dot(mixed[...], wm[...])
    res_ref[...] = residual
    xhat2, _ = norm_parts(residual)
    h2_ref[...] = (xhat2 * gains[1:2]).astype(bf16)
    for c in outs:
        c.wait()


def started(pairs, sems):
    copies = [pltpu.make_async_copy(a, b, sems.at[i]) for i, (a, b) in enumerate(pairs)]
    for c in copies:
        c.start()
    return copies


def gated_kernel(
    h2_hbm, gt_hbm, perm0, perm1, perm2, gtt0, gtt1, gtt2, w_hbm,
    branch_ref, gh2_ref, sib0, sib1, sib2, own0, own1, own2,
    h2, gt, perm, gtt, w, gate, up, gh, hid, gg, gu, h2t, grads, sems, out_sems,
):
    pairs = [(h2_hbm, h2)]
    for j, (p, g) in enumerate(((perm0, gtt0), (perm1, gtt1), (perm2, gtt2))):
        base = FF_AT + j * 3 * CW
        pairs += [
            (w_hbm.at[:, pl.ds(base + i * CW, CW)], w.at[j, :, pl.ds(i * CW, CW)]) for i in range(3)
        ]
        pairs += [(p, perm.at[j]), (g, gtt.at[j])]
        if j == 0:
            pairs.append((gt_hbm, gt))
    copies = iter(started(pairs, sems))
    next(copies).wait()
    size = 16

    def rows(i, carry):
        r = pl.ds(pl.multiple_of(i * size, size), size)
        g, u, d = gate[r, :], up[r, :], gh[r, :]
        cdf = 0.5 * (1.0 + lax.erf(g * (0.5**0.5)))
        act = g * cdf
        slope = cdf + g * (jnp.exp(-0.5 * g * g) * 0.3989422804014327)
        hid[r, :] = (act * u).astype(bf16)
        gg[r, :] = (d * u * slope).astype(bf16)
        gu[r, :] = (d * act).astype(bf16)
        return carry

    outs = []
    for j, targets in enumerate(((sib0, own0), (sib1, own1), (sib2, own2))):
        next(copies).wait()
        gate[...] = dot(h2[...], w[j, :, :CW])
        next(copies).wait()
        up[...] = dot(h2[...], w[j, :, CW : 2 * CW])
        for _ in range(4 if j == 0 else 3):
            next(copies).wait()
        gh[...] = dot(gt[...], w[j, :, 2 * CW :])
        h2t[...] = dot_t(perm[j], h2[...]).astype(bf16)
        lax.fori_loop(0, gate.shape[0] // size, rows, 0)
        for half, to in enumerate(targets):
            rows_at = pl.ds(half * ROWS, ROWS)
            for i, (left, right) in enumerate(((h2t, gg), (h2t, gu), (gtt.at[j], hid))):
                cols = pl.ds(i * CW, CW)
                grads[j, rows_at, cols] = dot(left[rows_at, :], right[...]).astype(bf16)
                outs.append(
                    pltpu.make_async_copy(
                        grads.at[j, rows_at, cols], to.at[:, cols], out_sems.at[6 * j + 3 * half + i]
                    )
                )
                outs[-1].start()
        more = dot_t(hid[...], w[j, :, 2 * CW :])
        more_gh2 = dot_t(gg[...], w[j, :, :CW]) + dot_t(gu[...], w[j, :, CW : 2 * CW])
        branch_ref[...] = more if j == 0 else branch_ref[...] + more
        gh2_ref[...] = more_gh2 if j == 0 else gh2_ref[...] + more_gh2
    for c in outs:
        c.wait()


def back_kernel(
    gain_ref, seg_ref, cos_ref, sin_ref, gt_ref, res_hbm, branch_hbm, gh2_hbm, qkv_hbm, prob_hbm,
    h1_hbm, mixed_hbm, tok_hbm, perm0, perm1, perm2, w_hbm,
    out_ref, gin_ref, sib0, sib1, sib2, own0, own1, own2,
    res_ref, branch_ref, gh2_ref, qkv, prob, h1, mixed, tok, p0, p1, p2, wp, wm,
    gr, ga_ref, gm, gp, h1t, mt, grads, sems, out_sems,
):
    perms = (p0, p1, p2)
    copies = started(
        [
            (res_hbm, res_ref), (branch_hbm, branch_ref), (gh2_hbm, gh2_ref),
            (w_hbm.at[:, pl.ds(MIX_AT, D)], wm), (qkv_hbm, qkv), (prob_hbm, prob),
            (h1_hbm, h1), (mixed_hbm, mixed), (perm0, p0), (perm1, p1), (perm2, p2),
            (w_hbm.at[:, pl.ds(0, 3 * D)], wp), (tok_hbm, tok),
        ],
        sems,
    )
    for c in copies[:3]:
        c.wait()
    residual = res_ref[...]
    live = seg_ref[...] < 4
    out_ref[...] = jnp.where(live, residual + branch_ref[...], 0.0).astype(bf16)
    xhat2, r2 = norm_parts(residual)
    gh2 = gh2_ref[...]
    second = jnp.sum(gh2 * xhat2, axis=0, keepdims=True)
    n = gh2 * gain_ref[1:2]
    spread = jnp.mean(n * xhat2, axis=-1, keepdims=True)
    grad_res = gt_ref[...].astype(f32) + r2 * (
        n - jnp.mean(n, axis=-1, keepdims=True) - xhat2 * spread
    )
    gr[...] = grad_res
    ga = grad_res.astype(bf16)
    ga_ref[...] = ga
    copies[3].wait()
    gm[...] = dot_t(ga, wm[...]).astype(bf16)
    copies[4].wait()
    copies[5].wait()
    low_half = lax.broadcasted_iota(jnp.int32, (1, PAIR), 1) % HD < HD // 2
    first = lax.broadcasted_iota(jnp.int32, (1, PAIR), 1) < HD
    zero = jnp.zeros((), bf16)

    def pair(p):
        cos, sin = cos_ref[...], sin_ref[...]
        q = qkv[:, pair_slice(p)]
        k = qkv[:, pair_slice(p, D)]
        v = qkv[:, pair_slice(p, 2 * D)]
        g = gm[:, pair_slice(p)]
        dq, dk, dv = [], [], []
        for side in range(2):
            mine = first if side == 0 else jnp.logical_not(first)
            probs = prob[2 * p + side]
            grad_probs = dot_t(jnp.where(mine, g, zero), v)
            weighted = probs * grad_probs
            delta = jnp.sum(weighted, axis=-1, keepdims=True)
            gs = (weighted - probs * delta).astype(bf16)
            dq.append(dot(gs, k))
            dk.append(dot_first(gs, q))
            dv.append(dot_first(probs.astype(bf16), g))
        dq = jnp.where(first, dq[0], dq[1]) * (HD**-0.5)
        dk = jnp.where(first, dk[0], dk[1]) * (HD**-0.5)
        dv = jnp.where(first, dv[0], dv[1])
        gp[:, pair_slice(p)] = (dq * cos - half_swapped(dq, low_half) * sin).astype(bf16)
        gp[:, pair_slice(p, D)] = (dk * cos - half_swapped(dk, low_half) * sin).astype(bf16)
        gp[:, pair_slice(p, 2 * D)] = dv.astype(bf16)

    for p in range(PAIRS):
        pair(p)
    copies[6].wait()
    copies[7].wait()
    outs = []
    for j in range(CHUNKS):
        copies[8 + j].wait()
        h1t[...] = dot_t(perms[j][...], h1[...]).astype(bf16)
        mt[...] = dot_t(perms[j][...], mixed[...]).astype(bf16)
        lo, hi = MIX_CUTS[j]
        to = grads.at[j]
        to[:, pl.ds(0, D)] = dot(h1t[...], gp[:, j * D : (j + 1) * D]).astype(bf16)
        to[:, pl.ds(D, hi - lo)] = dot(mt[...], ga_ref[:, lo:hi]).astype(bf16)
        if j == CHUNKS - 1:
            copies[11].wait()
            copies[12].wait()
            gh1 = dot_t(gp[...], wp[...])
            xhat1, r1 = norm_parts(tok[...].astype(f32))
            one = jnp.sum(gh1 * xhat1, axis=0, keepdims=True)
            m = gh1 * gain_ref[0:1]
            spread = jnp.mean(m * xhat1, axis=-1, keepdims=True)
            gin_ref[...] = gr[...] + r1 * (m - jnp.mean(m, axis=-1, keepdims=True) - xhat1 * spread)
            row = lax.broadcasted_iota(jnp.int32, (128, D), 0)
            both = jnp.where(row == 0, one, jnp.where(row == 1, second, 0.0)).astype(bf16)
            to[:, pl.ds(D + 256, 128)] = dot_t(perms[j][...], both).astype(bf16)
        for half, group in enumerate(((sib0, sib1, sib2), (own0, own1, own2))):
            outs.append(
                pltpu.make_async_copy(
                    grads.at[j, pl.ds(half * ROWS, ROWS)], group[j], out_sems.at[2 * j + half]
                )
            )
            outs[-1].start()
    for c in outs:
        c.wait()


def turn_kernel(ff_terms, *refs):
    send, keep, whole = refs[ff_terms + 4 :]
    at = 0
    for terms in (refs[:ff_terms], refs[ff_terms : ff_terms + 4]):
        total = terms[0][...].astype(f32)
        for t in terms[1:]:
            total = total + t[...].astype(f32)
        whole[:, pl.ds(at, total.shape[1])] = total
        at += total.shape[1]
    send[...] = whole[pl.ds(0, 64), :].astype(bf16)
    keep[...] = whole[pl.ds(64, 64), :].astype(bf16)


def pack_kernel(packed, mixer, expand, reduce, gains, out, wide):
    out[:, pl.ds(0, MIX_AT)] = packed[...]
    out[:, pl.ds(MIX_AT, D)] = mixer[...]
    out[:, pl.ds(GAIN_AT, 128)] = gains[...]
    both = expand[...].astype(f32)
    wide[...] = jnp.zeros(wide.shape, f32)
    wide[0, :, pl.ds(0, FF)] = both[:, :FF]
    wide[1, :, pl.ds(0, FF)] = pltpu.roll(both, FF, 1)[:, :FF]
    wide[2, :, pl.ds(0, FF)] = reduce[...].astype(f32)
    for j in range(CHUNKS):
        for i in range(3):
            out[:, pl.ds(FF_AT + (3 * j + i) * CW, CW)] = wide[i, :, pl.ds(j * CW, CW)].astype(bf16)


def finish_kernel(*refs):
    gots, kepts = refs[:3], refs[3:6]
    packed, mixer, expand, reduce, gain, wide = refs[6:]
    ff = 3 * CW
    for j in range(CHUNKS):
        total = gots[j][...].astype(f32) + kepts[j][...].astype(f32)
        for i in range(3):
            wide[i, :, pl.ds(j * CW, CW)] = total[:, i * CW : (i + 1) * CW]
        packed[:, pl.ds(j * D, D)] = total[:, ff : ff + D]
        lo, hi = MIX_CUTS[j]
        mixer[:, pl.ds(lo, hi - lo)] = total[:, ff + D : ff + D + hi - lo]
    gain[...] = jnp.transpose(total[:, ff + D + 256 :])[:8]
    reduce[...] = wide[2, :, pl.ds(0, FF)]
    lane = lax.broadcasted_iota(jnp.int32, (1, 2 * FF), 1)
    pad = jnp.zeros((8, 2 * FF - CHUNKS * CW), f32)
    gate = jnp.concatenate([wide[0], pad], axis=1)
    up = pltpu.roll(jnp.concatenate([wide[1], pad], axis=1), FF, 1)
    expand[...] = jnp.where(lane < FF, gate, up)


def arr(shape, dtype):
    return jax.ShapeDtypeStruct(shape, dtype)


VSPEC = pl.BlockSpec(memory_space=pltpu.VMEM)
HSPEC = pl.BlockSpec(memory_space=pl.ANY)
DMA = pltpu.SemaphoreType.DMA


def run(
    kernel, name, inputs, out_shape, scratch=(), in_hbm=(), out_hbm=(), after=(), through=(), specs=()
):
    count, outs, extra = len(inputs), len(out_shape), len(after) + len(through)

    def with_order(*refs):
        rest = refs[count + extra :]
        kernel(*refs[:count], *rest[:outs], *rest[outs + len(through) :])

    return pl.pallas_call(
        with_order,
        out_shape=tuple(out_shape) + tuple(arr(t.shape, t.dtype) for t in through),
        grid=(1,) if specs else (),
        in_specs=(list(specs) or [HSPEC if i in in_hbm else VSPEC for i in range(count)])
        + [HSPEC] * extra,
        out_specs=tuple(HSPEC if i in out_hbm else VSPEC for i in range(outs))
        + (HSPEC,) * len(through),
        input_output_aliases={count + len(after) + i: outs + i for i in range(len(through))},
        scratch_shapes=list(scratch),
        compiler_params=pltpu.CompilerParams(vmem_limit_bytes=VMEM),
        cost_estimate=pl.CostEstimate(flops=10**14, bytes_accessed=1024, transcendentals=0),
        name=name,
    )(*inputs, *after, *through)


def token_layout(lengths, slot_count):
    places = jnp.arange(slot_count, dtype=jnp.int32)
    ends = jnp.cumsum(lengths)
    starts = ends - lengths
    segment = jnp.sum((places[:, None] >= ends[None, :]).astype(jnp.int32), axis=1)
    live = places < ends[-1]
    picked = (segment[:, None] == jnp.arange(lengths.shape[0], dtype=jnp.int32)[None, :]).astype(
        jnp.int32
    )
    position = jnp.where(live, places - jnp.sum(picked * starts[None, :], axis=1), 0)
    segment = jnp.where(live, segment, lengths.shape[0] + places)
    return segment, position


def rotary_tables(position):
    frequency = rope_base ** (-(jnp.arange(HD // 2, dtype=f32) * 2.0 / HD))
    angles = position.astype(f32)[:, None] * frequency
    cos, sin = jnp.cos(angles), jnp.sin(angles)
    return (
        jnp.concatenate([cos, cos, cos, cos], axis=-1),
        jnp.concatenate([-sin, sin, -sin, sin], axis=-1),
    )


ORDERS = (("x", "y", "z"), ("y", "z", "x"), ("z", "x", "y"))


def hops(core):
    return (1, 3) if core == 0 else (3, 1)


def row_order(order):
    core = lax.axis_index("c")
    row = jnp.arange(D, dtype=jnp.int32)
    mine, inner = row >= ROWS, row % ROWS
    side = jnp.where(mine, core, 1 - core)
    place = {}
    for axis, size in zip(order, (128, 32, 8)):
        turn = inner // size % 4
        apart = jnp.where(turn == 0, 2, jnp.where(turn == 3, 0, jnp.where((turn == 1) == (side == 0), 1, 3)))
        place[axis] = lax.axis_index(axis) ^ apart
    feature = ((place["y"] * 4 + place["z"]) * 4 + place["x"]) * 16 + side * 8 + inner % 8
    return (feature[:, None] == jnp.arange(D, dtype=jnp.int32)[None, :]).astype(bf16)


def to_partner(a, axis, step):
    pairs = [(i * 2 + c, (i ^ hops(c)[step]) * 2 + c) for i in range(4) for c in range(2)]
    return lax.ppermute(a, (axis, "c"), pairs)


def to_sibling(a):
    return lax.ppermute(a, "c", [(0, 1), (1, 0)])


def added(*arrays):
    total = arrays[0]
    for a in arrays[1:]:
        total = total + a
    return total


class PartSum:
    def __init__(self, order, sib, own):
        self.axis = order[0]
        self.own, self.arrived = own, to_sibling(sib)
        self.lo, self.step, self.got = 0, 0, None

    def piece(self, lo, rows):
        at = slice(lo, lo + rows)
        terms = [self.own[at], self.arrived[at]]
        if self.got is not None:
            terms.append(self.got[lo - self.lo : lo - self.lo + rows])
        return added(*terms)

    def send(self):
        rows = (ROWS - self.lo) // 2
        out = self.piece(self.lo, rows)
        got = to_partner(out, self.axis, self.step)
        self.got = got if self.got is None else (got, self.got)
        self.lo += rows
        self.step += 1
        return out

    def last_terms(self):
        cols = self.own.shape[1]
        got, kept = self.got
        specs = [pl.BlockSpec((128, cols), lambda i, at=at: (at, 0)) for at in (3, 3, 0, 1)]
        return (self.own, self.arrived, got, kept), specs

    def total(self):
        got, kept = self.got
        at = slice(self.lo, ROWS)
        return (added(self.own[at], self.arrived[at], got, kept[ROWS // 4 :]),), [VSPEC]


def halves(a):
    n = a.shape[0] // 2
    return a[:n], a[n:]


def local_step(tokens, cotangent, lengths, weights, perms, part_sum):
    n = tokens.shape[0]
    segment, position = token_layout(lengths, n)
    cos, sin = rotary_tables(position)
    seg_col, seg_row = segment[:, None], segment[None, :]
    tile = arr((n, D), bf16)
    wide = arr((n, D), f32)
    vm = pltpu.VMEM
    gt, *gtts = run(
        cotangent_kernel, "cotangent", (cotangent, seg_col, *perms),
        (tile,) + (arr((D, n), bf16),) * CHUNKS,
    )
    qkv, probs, residual, h1, h2, mixed, gains = run(
        attend_kernel, "attend", (tokens, seg_col, seg_row, cos, sin, weights),
        (arr((n, 3 * D), bf16), arr((H, n, n), f32), wide, tile, tile, tile, arr((8, D), f32)),
        [
            vm((D, 3 * D), bf16), vm((D, D), bf16), vm((D, 128), bf16), vm((n, 3 * D), f32),
            vm((n, n), f32), vm((n, 3 * D), bf16), vm((H, n, n), f32), DMA((3,)), DMA((3,)),
        ],
        in_hbm=(5,),
        out_hbm=(0, 1),
    )
    branch, gh2, *pieces = run(
        gated_kernel, "gated", (h2, gt, *perms, *gtts, weights),
        (wide, wide) + (arr((ROWS, 3 * CW), bf16),) * 6,
        [vm((n, D), bf16), vm((n, D), bf16), vm((3, D, D), bf16), vm((3, D, n), bf16)]
        + [vm((3, D, 3 * CW), bf16)]
        + [vm((n, CW), f32)] * 3
        + [vm((n, CW), bf16)] * 3
        + [vm((D, n), bf16), vm((3, D, 3 * CW), bf16), DMA((17,)), DMA((18,))],
        in_hbm=range(9),
        out_hbm=range(2, 8),
    )
    ff = [part_sum(ORDERS[j], pieces[j], pieces[3 + j]) for j in range(CHUNKS)]
    after = ()
    for f in ff:
        if after:
            f.own, _ = lax.optimization_barrier((f.own, after[-1]))
        after += (f.send(),)
    block_output, input_grad, *pieces = run(
        back_kernel, "back",
        (gains, seg_col, cos, sin, gt, residual, branch, gh2, qkv, probs, h1, mixed, tokens, *perms, weights),
        (tile, wide) + (arr((ROWS, A_COLS), bf16),) * 6,
        [vm((n, D), f32)] * 3
        + [vm((n, 3 * D), bf16), vm((H, n, n), f32)]
        + [vm((n, D), bf16)] * 3
        + [vm((D, D), bf16)] * 3
        + [vm((D, 3 * D), bf16), vm((D, D), bf16), vm((n, D), f32), vm((n, D), bf16), vm((n, D), bf16)]
        + [vm((n, 3 * D), bf16), vm((D, n), bf16), vm((D, n), bf16), vm((3, D, A_COLS), bf16)]
        + [DMA((13,)), DMA((6,))],
        in_hbm=range(5, 17),
        out_hbm=range(2, 8),
        after=after,
        through=tuple(f.own for f in ff),
    )
    for f, own in zip(ff, pieces[6:]):
        f.own = own
    att = [part_sum(ORDERS[j], pieces[j], pieces[3 + j]) for j in range(CHUNKS)]
    return block_output, input_grad, ff, att


def summed(ff, att):
    for f in ff:
        f.send()
    for f, a in zip(ff, att):
        f.own, _ = lax.optimization_barrier((f.own, a.send()))
    for a in att:
        a.send()
    pairs = []
    for f, a in zip(ff, att):
        f_terms, f_specs = f.total()
        a_terms, a_specs = a.last_terms()
        cols = f.own.shape[1] + a.own.shape[1]
        pairs.append(
            run(
                functools.partial(turn_kernel, len(f_terms)), "turn", f_terms + a_terms, (arr((64, cols), bf16),) * 2,
                [pltpu.VMEM((128, cols), f32)], specs=f_specs + a_specs,
            )
        )
    for ring, step in ((1, 0), (1, 1), (2, 0), (2, 1)):
        gots = [to_partner(p[0], order[ring], step) for p, order in zip(pairs, ORDERS)]
        kept = [p[1] for p in pairs]
        if (ring, step) != (2, 1):
            pairs = [halves(added(g, k)) for g, k in zip(gots, kept)]
    return gots, kept


def own_rows(gots, kept):
    n = 8
    *grads, gains = run(
        finish_kernel, "finish", (*gots, *kept),
        tuple(arr((n, c), f32) for c in (3 * D, D, 2 * FF, FF, 8)),
        [pltpu.VMEM((3, n, CHUNKS * CW), f32)],
    )
    return (*grads, gains[0], gains[1])


def body(
    tokens, packed_proj, mixer_proj, expand_proj, reduce_proj, first_gain, second_gain,
    sequence_lengths, cotangent,
):
    gains = jnp.pad(jnp.stack([first_gain, second_gain], axis=1), ((0, 0), (0, 126)))
    (shard,) = run(
        pack_kernel, "pack", (packed_proj, mixer_proj, expand_proj, reduce_proj, gains),
        (arr((8, W_COLS), bf16),), [pltpu.VMEM((3, 8, CHUNKS * CW), f32)],
    )
    weights = lax.all_gather(shard, ALL, axis=0, tiled=True)
    perms = [row_order(order) for order in ORDERS]
    block_output, input_grad, ff, att = local_step(
        tokens, cotangent, sequence_lengths, weights, perms, PartSum
    )
    return (block_output, input_grad, *own_rows(*summed(ff, att)))


def solution(mesh):
    torus = Mesh(mesh.devices.reshape(4, 4, 4, 2), ALL)
    row, flat = P(ALL, None), P(ALL)
    return jax.shard_map(
        body,
        mesh=torus,
        in_specs=(row,) * 5 + (flat, flat, flat, row),
        out_specs=(row,) * 6 + (flat, flat),
        check_vma=False,
    )
```

```python
import functools

import jax
import jax.numpy as jnp
from jax import lax
from jax.experimental import pallas as pl
from jax.experimental.pallas import tpu as pltpu
from jax.sharding import Mesh
from jax.sharding import PartitionSpec as P

H = 16
HD = 64
PAIR = 2 * HD
PAIRS = H // 2
epsilon = 1e-05
rope_base = 160000.0
masked_score = -1e30
AXES = ("y", "z", "x")
ALL = ("y", "z", "x", "c")
VMEM = 60 * 1024 * 1024
bf16 = jnp.bfloat16
f32 = jnp.float32

D = 1024
FF = 2624
CHUNKS = 3
CW = 896
MIX_AT = 3 * D
GAIN_AT = 4 * D
FF_AT = 4 * D + 128
W_COLS = FF_AT + CHUNKS * 3 * CW
ROWS = 512
MIX_CUTS = ((0, 384), (384, 768), (768, 1024))
A_COLS = D + 384


def dot(a, b):
    return lax.dot_general(a, b, (((1,), (0,)), ((), ())), preferred_element_type=f32)


def dot_t(a, b):
    return lax.dot_general(a, b, (((1,), (1,)), ((), ())), preferred_element_type=f32)


def dot_first(a, b):
    return lax.dot_general(a, b, (((0,), (0,)), ((), ())), preferred_element_type=f32)


def norm_parts(values):
    centered = values - jnp.mean(values, axis=-1, keepdims=True)
    scale = lax.rsqrt(jnp.mean(centered * centered, axis=-1, keepdims=True) + epsilon)
    return centered * scale, scale


def half_swapped(v, low_half):
    return jnp.where(low_half, pltpu.roll(v, PAIR - HD // 2, 1), pltpu.roll(v, HD // 2, 1))


def pair_slice(p, at=0):
    return pl.ds(p * PAIR + at, PAIR)


def cotangent_kernel(cot_ref, seg_ref, *refs):
    perms, gt_ref, gtts = refs[:CHUNKS], refs[CHUNKS], refs[CHUNKS + 1 :]
    gt = jnp.where(seg_ref[...] < 4, cot_ref[...].astype(f32), 0.0).astype(bf16)
    gt_ref[...] = gt
    for perm, gtt in zip(perms, gtts):
        gtt[...] = dot_t(perm[...], gt).astype(bf16)


def attend_kernel(
    tok_ref, seg_ref, segt_ref, cos_ref, sin_ref, w_ref,
    qkv_hbm, prob_hbm, res_ref, h1_ref, h2_ref, mixed, gain_ref,
    wp, wm, wg, packed, bias, qkv, prob, sems, out_sems,
):
    copies = [
        pltpu.make_async_copy(w_ref.at[:, pl.ds(GAIN_AT, 128)], wg, sems.at[0]),
        pltpu.make_async_copy(w_ref.at[:, pl.ds(0, 3 * D)], wp, sems.at[1]),
        pltpu.make_async_copy(w_ref.at[:, pl.ds(MIX_AT, D)], wm, sems.at[2]),
    ]
    for c in copies:
        c.start()
    tokens = tok_ref[...].astype(f32)
    xhat, _ = norm_parts(tokens)
    bias[...] = jnp.where(seg_ref[...] == segt_ref[...], 0.0, masked_score)
    copies[0].wait()
    gains = jnp.transpose(wg[...].astype(f32))[:8]
    gain_ref[...] = gains
    h1 = (xhat * gains[0:1]).astype(bf16)
    h1_ref[...] = h1
    copies[1].wait()
    packed[...] = dot(h1, wp[...])
    low_half = lax.broadcasted_iota(jnp.int32, (1, PAIR), 1) % HD < HD // 2
    first = lax.broadcasted_iota(jnp.int32, (1, PAIR), 1) < HD
    zero = jnp.zeros((), bf16)

    def pair(p):
        cos, sin = cos_ref[...], sin_ref[...]
        q = packed[:, pair_slice(p)]
        k = packed[:, pair_slice(p, D)]
        q = (q * cos + half_swapped(q, low_half) * sin).astype(bf16)
        k = (k * cos + half_swapped(k, low_half) * sin).astype(bf16)
        v = packed[:, pair_slice(p, 2 * D)].astype(bf16)
        qkv[:, pair_slice(p)] = q
        qkv[:, pair_slice(p, D)] = k
        qkv[:, pair_slice(p, 2 * D)] = v
        outs = []
        for side in range(2):
            mine = first if side == 0 else jnp.logical_not(first)
            scores = dot_t(jnp.where(mine, q, zero), k) * (HD**-0.5) + bias[...]
            top = jnp.max(scores, axis=-1, keepdims=True)
            e = jnp.exp(scores - top)
            probs = e * (1.0 / jnp.sum(e, axis=-1, keepdims=True))
            prob[2 * p + side] = probs
            outs.append(dot(probs.astype(bf16), v))
        mixed[:, pair_slice(p)] = jnp.where(first, outs[0], outs[1]).astype(bf16)

    outs = []
    for i in range(2):
        for p in range(i * PAIRS // 2, (i + 1) * PAIRS // 2):
            pair(p)
        part = pl.ds(i * PAIRS, PAIRS)
        outs.append(pltpu.make_async_copy(prob.at[part], prob_hbm.at[part], out_sems.at[i]))
        outs[-1].start()
    outs.append(pltpu.make_async_copy(qkv, qkv_hbm, out_sems.at[2]))
    outs[-1].start()
    copies[2].wait()
    residual = tokens + dot(mixed[...], wm[...])
    res_ref[...] = residual
    xhat2, _ = norm_parts(residual)
    h2_ref[...] = (xhat2 * gains[1:2]).astype(bf16)
    for c in outs:
        c.wait()


def started(pairs, sems):
    copies = [pltpu.make_async_copy(a, b, sems.at[i]) for i, (a, b) in enumerate(pairs)]
    for c in copies:
        c.start()
    return copies


def in_part_order(order_ref, part, rows, tmp):
    for r in range(D // 8):
        at = pl.multiple_of(order_ref[part * (D // 8) + r], 8)
        tmp[pl.ds(8 * r, 8), :] = rows[pl.ds(at, 8), :]
    return tmp[...].astype(bf16)


def gated_kernel(
    order_ref, h2_hbm, gt_hbm, gtt0, gtt1, gtt2, w_hbm,
    branch_ref, gh2_ref, sib0, sib1, sib2, own0, own1, own2,
    h2, gt, gtt, w, gate, up, gh, hid, gg, gu, turned, tmp, h2t, grads, sems, out_sems,
):
    pairs = [(h2_hbm, h2)]
    for j, g in enumerate((gtt0, gtt1, gtt2)):
        base = FF_AT + j * 3 * CW
        pairs += [
            (w_hbm.at[:, pl.ds(base + i * CW, CW)], w.at[j, :, pl.ds(i * CW, CW)]) for i in range(3)
        ]
        pairs.append((g, gtt.at[j]))
        if j == 0:
            pairs.append((gt_hbm, gt))
    copies = iter(started(pairs, sems))
    next(copies).wait()
    size = 16

    def rows(i, carry):
        r = pl.ds(pl.multiple_of(i * size, size), size)
        g, u, d = gate[r, :], up[r, :], gh[r, :]
        cdf = 0.5 * (1.0 + lax.erf(g * (0.5**0.5)))
        act = g * cdf
        slope = cdf + g * (jnp.exp(-0.5 * g * g) * 0.3989422804014327)
        hid[r, :] = (act * u).astype(bf16)
        gg[r, :] = (d * u * slope).astype(bf16)
        gu[r, :] = (d * act).astype(bf16)
        return carry

    outs = []
    for j, targets in enumerate(((sib0, own0), (sib1, own1), (sib2, own2))):
        next(copies).wait()
        gate[...] = dot(h2[...], w[j, :, :CW])
        next(copies).wait()
        up[...] = dot(h2[...], w[j, :, CW : 2 * CW])
        for _ in range(3 if j == 0 else 2):
            next(copies).wait()
        gh[...] = dot(gt[...], w[j, :, 2 * CW :])
        if j == 0:
            turned[...] = jnp.transpose(h2[...].astype(f32))
        h2t[...] = in_part_order(order_ref, j, turned, tmp)
        lax.fori_loop(0, gate.shape[0] // size, rows, 0)
        for half, to in enumerate(targets):
            rows_at = pl.ds(half * ROWS, ROWS)
            for i, (left, right) in enumerate(((h2t, gg), (h2t, gu), (gtt.at[j], hid))):
                cols = pl.ds(i * CW, CW)
                grads[j, rows_at, cols] = dot(left[rows_at, :], right[...]).astype(bf16)
                outs.append(
                    pltpu.make_async_copy(
                        grads.at[j, rows_at, cols], to.at[:, cols], out_sems.at[6 * j + 3 * half + i]
                    )
                )
                outs[-1].start()
        more = dot_t(hid[...], w[j, :, 2 * CW :])
        more_gh2 = dot_t(gg[...], w[j, :, :CW]) + dot_t(gu[...], w[j, :, CW : 2 * CW])
        branch_ref[...] = more if j == 0 else branch_ref[...] + more
        gh2_ref[...] = more_gh2 if j == 0 else gh2_ref[...] + more_gh2
    for c in outs:
        c.wait()


def back_kernel(
    gain_ref, seg_ref, cos_ref, sin_ref, gt_ref, res_hbm, branch_hbm, gh2_hbm, qkv_hbm, prob_hbm,
    h1_hbm, mixed_hbm, tok_hbm, w_hbm, order_ref,
    out_ref, gin_ref, sib0, sib1, sib2, own0, own1, own2,
    res_ref, branch_ref, gh2_ref, qkv, prob, h1, mixed, tok, wp, wm,
    gr, ga_ref, gm, gp, h1_turned, mixed_turned, gains_turned, tmp, gains_tmp,
    h1t, mt, grads, sems, out_sems,
):
    copies = started(
        [
            (res_hbm, res_ref), (branch_hbm, branch_ref), (gh2_hbm, gh2_ref),
            (w_hbm.at[:, pl.ds(MIX_AT, D)], wm), (qkv_hbm, qkv), (prob_hbm, prob),
            (h1_hbm, h1), (mixed_hbm, mixed),
            (w_hbm.at[:, pl.ds(0, 3 * D)], wp), (tok_hbm, tok),
        ],
        sems,
    )
    for c in copies[:3]:
        c.wait()
    residual = res_ref[...]
    live = seg_ref[...] < 4
    out_ref[...] = jnp.where(live, residual + branch_ref[...], 0.0).astype(bf16)
    xhat2, r2 = norm_parts(residual)
    gh2 = gh2_ref[...]
    second = jnp.sum(gh2 * xhat2, axis=0, keepdims=True)
    n = gh2 * gain_ref[1:2]
    spread = jnp.mean(n * xhat2, axis=-1, keepdims=True)
    grad_res = gt_ref[...].astype(f32) + r2 * (
        n - jnp.mean(n, axis=-1, keepdims=True) - xhat2 * spread
    )
    gr[...] = grad_res
    ga = grad_res.astype(bf16)
    ga_ref[...] = ga
    copies[3].wait()
    gm[...] = dot_t(ga, wm[...]).astype(bf16)
    copies[4].wait()
    copies[5].wait()
    low_half = lax.broadcasted_iota(jnp.int32, (1, PAIR), 1) % HD < HD // 2
    first = lax.broadcasted_iota(jnp.int32, (1, PAIR), 1) < HD
    zero = jnp.zeros((), bf16)

    def pair(p):
        cos, sin = cos_ref[...], sin_ref[...]
        q = qkv[:, pair_slice(p)]
        k = qkv[:, pair_slice(p, D)]
        v = qkv[:, pair_slice(p, 2 * D)]
        g = gm[:, pair_slice(p)]
        dq, dk, dv = [], [], []
        for side in range(2):
            mine = first if side == 0 else jnp.logical_not(first)
            probs = prob[2 * p + side]
            grad_probs = dot_t(jnp.where(mine, g, zero), v)
            weighted = probs * grad_probs
            delta = jnp.sum(weighted, axis=-1, keepdims=True)
            gs = (weighted - probs * delta).astype(bf16)
            dq.append(dot(gs, k))
            dk.append(dot_first(gs, q))
            dv.append(dot_first(probs.astype(bf16), g))
        dq = jnp.where(first, dq[0], dq[1]) * (HD**-0.5)
        dk = jnp.where(first, dk[0], dk[1]) * (HD**-0.5)
        dv = jnp.where(first, dv[0], dv[1])
        gp[:, pair_slice(p)] = (dq * cos - half_swapped(dq, low_half) * sin).astype(bf16)
        gp[:, pair_slice(p, D)] = (dk * cos - half_swapped(dk, low_half) * sin).astype(bf16)
        gp[:, pair_slice(p, 2 * D)] = dv.astype(bf16)

    for p in range(PAIRS):
        pair(p)
    copies[6].wait()
    copies[7].wait()
    h1_turned[...] = jnp.transpose(h1[...].astype(f32))
    mixed_turned[...] = jnp.transpose(mixed[...].astype(f32))
    outs = []
    for j in range(CHUNKS):
        h1t[...] = in_part_order(order_ref, j, h1_turned, tmp)
        mt[...] = in_part_order(order_ref, j, mixed_turned, tmp)
        lo, hi = MIX_CUTS[j]
        to = grads.at[j]
        to[:, pl.ds(0, D)] = dot(h1t[...], gp[:, j * D : (j + 1) * D]).astype(bf16)
        to[:, pl.ds(D, hi - lo)] = dot(mt[...], ga_ref[:, lo:hi]).astype(bf16)
        if j == CHUNKS - 1:
            copies[8].wait()
            copies[9].wait()
            gh1 = dot_t(gp[...], wp[...])
            xhat1, r1 = norm_parts(tok[...].astype(f32))
            one = jnp.sum(gh1 * xhat1, axis=0, keepdims=True)
            m = gh1 * gain_ref[0:1]
            spread = jnp.mean(m * xhat1, axis=-1, keepdims=True)
            gin_ref[...] = gr[...] + r1 * (m - jnp.mean(m, axis=-1, keepdims=True) - xhat1 * spread)
            row = lax.broadcasted_iota(jnp.int32, (128, D), 0)
            both = jnp.where(row == 0, one, jnp.where(row == 1, second, 0.0))
            gains_turned[...] = jnp.transpose(both)
            to[:, pl.ds(D + 256, 128)] = in_part_order(order_ref, j, gains_turned, gains_tmp)
        for half, group in enumerate(((sib0, sib1, sib2), (own0, own1, own2))):
            outs.append(
                pltpu.make_async_copy(
                    grads.at[j, pl.ds(half * ROWS, ROWS)], group[j], out_sems.at[2 * j + half]
                )
            )
            outs[-1].start()
    for c in outs:
        c.wait()


def turn_kernel(ff_terms, *refs):
    send, keep, whole = refs[ff_terms + 4 :]
    at = 0
    for terms in (refs[:ff_terms], refs[ff_terms : ff_terms + 4]):
        total = terms[0][...].astype(f32)
        for t in terms[1:]:
            total = total + t[...].astype(f32)
        whole[:, pl.ds(at, total.shape[1])] = total
        at += total.shape[1]
    send[...] = whole[pl.ds(0, 64), :].astype(bf16)
    keep[...] = whole[pl.ds(64, 64), :].astype(bf16)


def pack_kernel(packed, mixer, expand, reduce, gains, out, wide):
    out[:, pl.ds(0, MIX_AT)] = packed[...]
    out[:, pl.ds(MIX_AT, D)] = mixer[...]
    out[:, pl.ds(GAIN_AT, 128)] = gains[...]
    both = expand[...].astype(f32)
    wide[...] = jnp.zeros(wide.shape, f32)
    wide[0, :, pl.ds(0, FF)] = both[:, :FF]
    wide[1, :, pl.ds(0, FF)] = pltpu.roll(both, FF, 1)[:, :FF]
    wide[2, :, pl.ds(0, FF)] = reduce[...].astype(f32)
    for j in range(CHUNKS):
        for i in range(3):
            out[:, pl.ds(FF_AT + (3 * j + i) * CW, CW)] = wide[i, :, pl.ds(j * CW, CW)].astype(bf16)


def finish_kernel(*refs):
    gots, kepts = refs[:3], refs[3:6]
    packed, mixer, expand, reduce, gain, wide = refs[6:]
    ff = 3 * CW
    for j in range(CHUNKS):
        total = gots[j][...].astype(f32) + kepts[j][...].astype(f32)
        for i in range(3):
            wide[i, :, pl.ds(j * CW, CW)] = total[:, i * CW : (i + 1) * CW]
        packed[:, pl.ds(j * D, D)] = total[:, ff : ff + D]
        lo, hi = MIX_CUTS[j]
        mixer[:, pl.ds(lo, hi - lo)] = total[:, ff + D : ff + D + hi - lo]
    gain[...] = jnp.transpose(total[:, ff + D + 256 :])[:8]
    reduce[...] = wide[2, :, pl.ds(0, FF)]
    lane = lax.broadcasted_iota(jnp.int32, (1, 2 * FF), 1)
    pad = jnp.zeros((8, 2 * FF - CHUNKS * CW), f32)
    gate = jnp.concatenate([wide[0], pad], axis=1)
    up = pltpu.roll(jnp.concatenate([wide[1], pad], axis=1), FF, 1)
    expand[...] = jnp.where(lane < FF, gate, up)


def arr(shape, dtype):
    return jax.ShapeDtypeStruct(shape, dtype)


VSPEC = pl.BlockSpec(memory_space=pltpu.VMEM)
HSPEC = pl.BlockSpec(memory_space=pl.ANY)
SSPEC = pl.BlockSpec(memory_space=pltpu.SMEM)
DMA = pltpu.SemaphoreType.DMA


def run(
    kernel, name, inputs, out_shape, scratch=(), in_hbm=(), out_hbm=(), after=(), through=(), specs=(),
    in_smem=(),
):
    count, outs, extra = len(inputs), len(out_shape), len(after) + len(through)

    def with_order(*refs):
        rest = refs[count + extra :]
        kernel(*refs[:count], *rest[:outs], *rest[outs + len(through) :])

    return pl.pallas_call(
        with_order,
        out_shape=tuple(out_shape) + tuple(arr(t.shape, t.dtype) for t in through),
        grid=(1,) if specs else (),
        in_specs=(
            list(specs)
            or [HSPEC if i in in_hbm else SSPEC if i in in_smem else VSPEC for i in range(count)]
        )
        + [HSPEC] * extra,
        out_specs=tuple(HSPEC if i in out_hbm else VSPEC for i in range(outs))
        + (HSPEC,) * len(through),
        input_output_aliases={count + len(after) + i: outs + i for i in range(len(through))},
        scratch_shapes=list(scratch),
        compiler_params=pltpu.CompilerParams(vmem_limit_bytes=VMEM),
        cost_estimate=pl.CostEstimate(flops=10**14, bytes_accessed=1024, transcendentals=0),
        name=name,
    )(*inputs, *after, *through)


def token_layout(lengths, slot_count):
    places = jnp.arange(slot_count, dtype=jnp.int32)
    ends = jnp.cumsum(lengths)
    starts = ends - lengths
    segment = jnp.sum((places[:, None] >= ends[None, :]).astype(jnp.int32), axis=1)
    live = places < ends[-1]
    picked = (segment[:, None] == jnp.arange(lengths.shape[0], dtype=jnp.int32)[None, :]).astype(
        jnp.int32
    )
    position = jnp.where(live, places - jnp.sum(picked * starts[None, :], axis=1), 0)
    segment = jnp.where(live, segment, lengths.shape[0] + places)
    return segment, position


def rotary_tables(position):
    frequency = rope_base ** (-(jnp.arange(HD // 2, dtype=f32) * 2.0 / HD))
    angles = position.astype(f32)[:, None] * frequency
    cos, sin = jnp.cos(angles), jnp.sin(angles)
    return (
        jnp.concatenate([cos, cos, cos, cos], axis=-1),
        jnp.concatenate([-sin, sin, -sin, sin], axis=-1),
    )


ORDERS = (("x", "y", "z"), ("y", "z", "x"), ("z", "x", "y"))


def hops(core):
    return (1, 3) if core == 0 else (3, 1)


def row_features(order):
    core = lax.axis_index("c")
    row = jnp.arange(D, dtype=jnp.int32)
    mine, inner = row >= ROWS, row % ROWS
    side = jnp.where(mine, core, 1 - core)
    place = {}
    for axis, size in zip(order, (128, 32, 8)):
        turn = inner // size % 4
        apart = jnp.where(turn == 0, 2, jnp.where(turn == 3, 0, jnp.where((turn == 1) == (side == 0), 1, 3)))
        place[axis] = lax.axis_index(axis) ^ apart
    return ((place["y"] * 4 + place["z"]) * 4 + place["x"]) * 16 + side * 8 + inner % 8


def row_order(order):
    return (row_features(order)[:, None] == jnp.arange(D, dtype=jnp.int32)[None, :]).astype(bf16)


def to_partner(a, axis, step):
    pairs = [(i * 2 + c, (i ^ hops(c)[step]) * 2 + c) for i in range(4) for c in range(2)]
    return lax.ppermute(a, (axis, "c"), pairs)


def to_sibling(a):
    return lax.ppermute(a, "c", [(0, 1), (1, 0)])


def added(*arrays):
    total = arrays[0]
    for a in arrays[1:]:
        total = total + a
    return total


class PartSum:
    def __init__(self, order, sib, own):
        self.axis = order[0]
        self.own, self.arrived = own, to_sibling(sib)
        self.lo, self.step, self.got = 0, 0, None

    def piece(self, lo, rows):
        at = slice(lo, lo + rows)
        terms = [self.own[at], self.arrived[at]]
        if self.got is not None:
            terms.append(self.got[lo - self.lo : lo - self.lo + rows])
        return added(*terms)

    def send(self):
        rows = (ROWS - self.lo) // 2
        out = self.piece(self.lo, rows)
        got = to_partner(out, self.axis, self.step)
        self.got = got if self.got is None else (got, self.got)
        self.lo += rows
        self.step += 1
        return out

    def last_terms(self):
        cols = self.own.shape[1]
        got, kept = self.got
        specs = [pl.BlockSpec((128, cols), lambda i, at=at: (at, 0)) for at in (3, 3, 0, 1)]
        return (self.own, self.arrived, got, kept), specs

    def total(self):
        got, kept = self.got
        at = slice(self.lo, ROWS)
        return (added(self.own[at], self.arrived[at], got, kept[ROWS // 4 :]),), [VSPEC]


def halves(a):
    n = a.shape[0] // 2
    return a[:n], a[n:]


def local_step(tokens, cotangent, lengths, weights, perms, part_sum):
    n = tokens.shape[0]
    segment, position = token_layout(lengths, n)
    cos, sin = rotary_tables(position)
    seg_col, seg_row = segment[:, None], segment[None, :]
    tile = arr((n, D), bf16)
    wide = arr((n, D), f32)
    vm = pltpu.VMEM
    orders = jnp.concatenate([row_features(order)[::8] for order in ORDERS])
    gt, *gtts = run(
        cotangent_kernel, "cotangent", (cotangent, seg_col, *perms),
        (tile,) + (arr((D, n), bf16),) * CHUNKS,
    )
    qkv, probs, residual, h1, h2, mixed, gains = run(
        attend_kernel, "attend", (tokens, seg_col, seg_row, cos, sin, weights),
        (arr((n, 3 * D), bf16), arr((H, n, n), f32), wide, tile, tile, tile, arr((8, D), f32)),
        [
            vm((D, 3 * D), bf16), vm((D, D), bf16), vm((D, 128), bf16), vm((n, 3 * D), f32),
            vm((n, n), f32), vm((n, 3 * D), bf16), vm((H, n, n), f32), DMA((3,)), DMA((3,)),
        ],
        in_hbm=(5,),
        out_hbm=(0, 1),
    )
    branch, gh2, *pieces = run(
        gated_kernel, "gated", (orders, h2, gt, *gtts, weights),
        (wide, wide) + (arr((ROWS, 3 * CW), bf16),) * 6,
        [vm((n, D), bf16), vm((n, D), bf16), vm((3, D, n), bf16)]
        + [vm((3, D, 3 * CW), bf16)]
        + [vm((n, CW), f32)] * 3
        + [vm((n, CW), bf16)] * 3
        + [vm((D, n), f32), vm((D, n), f32)]
        + [vm((D, n), bf16), vm((3, D, 3 * CW), bf16), DMA((14,)), DMA((18,))],
        in_hbm=range(1, 7),
        in_smem=(0,),
        out_hbm=range(2, 8),
    )
    ff = [part_sum(ORDERS[j], pieces[j], pieces[3 + j]) for j in range(CHUNKS)]
    after = ()
    for f in ff:
        if after:
            f.own, _ = lax.optimization_barrier((f.own, after[-1]))
        after += (f.send(),)
    block_output, input_grad, *pieces = run(
        back_kernel, "back",
        (gains, seg_col, cos, sin, gt, residual, branch, gh2, qkv, probs, h1, mixed, tokens, weights, orders),
        (tile, wide) + (arr((ROWS, A_COLS), bf16),) * 6,
        [vm((n, D), f32)] * 3
        + [vm((n, 3 * D), bf16), vm((H, n, n), f32)]
        + [vm((n, D), bf16)] * 3
        + [vm((D, 3 * D), bf16), vm((D, D), bf16), vm((n, D), f32), vm((n, D), bf16), vm((n, D), bf16)]
        + [vm((n, 3 * D), bf16), vm((D, n), f32), vm((D, n), f32), vm((D, 128), f32), vm((D, n), f32)]
        + [vm((D, 128), f32), vm((D, n), bf16), vm((D, n), bf16), vm((3, D, A_COLS), bf16)]
        + [DMA((10,)), DMA((6,))],
        in_hbm=range(5, 14),
        in_smem=(14,),
        out_hbm=range(2, 8),
        after=after,
        through=tuple(f.own for f in ff),
    )
    for f, own in zip(ff, pieces[6:]):
        f.own = own
    att = [part_sum(ORDERS[j], pieces[j], pieces[3 + j]) for j in range(CHUNKS)]
    return block_output, input_grad, ff, att


def summed(ff, att):
    for f in ff:
        f.send()
    for f, a in zip(ff, att):
        f.own, _ = lax.optimization_barrier((f.own, a.send()))
    for a in att:
        a.send()
    pairs = []
    for f, a in zip(ff, att):
        f_terms, f_specs = f.total()
        a_terms, a_specs = a.last_terms()
        cols = f.own.shape[1] + a.own.shape[1]
        pairs.append(
            run(
                functools.partial(turn_kernel, len(f_terms)), "turn", f_terms + a_terms, (arr((64, cols), bf16),) * 2,
                [pltpu.VMEM((128, cols), f32)], specs=f_specs + a_specs,
            )
        )
    for ring, step in ((1, 0), (1, 1), (2, 0), (2, 1)):
        gots = [to_partner(p[0], order[ring], step) for p, order in zip(pairs, ORDERS)]
        kept = [p[1] for p in pairs]
        if (ring, step) != (2, 1):
            pairs = [halves(added(g, k)) for g, k in zip(gots, kept)]
    return gots, kept


def own_rows(gots, kept):
    n = 8
    *grads, gains = run(
        finish_kernel, "finish", (*gots, *kept),
        tuple(arr((n, c), f32) for c in (3 * D, D, 2 * FF, FF, 8)),
        [pltpu.VMEM((3, n, CHUNKS * CW), f32)],
    )
    return (*grads, gains[0], gains[1])


def body(
    tokens, packed_proj, mixer_proj, expand_proj, reduce_proj, first_gain, second_gain,
    sequence_lengths, cotangent,
):
    gains = jnp.pad(jnp.stack([first_gain, second_gain], axis=1), ((0, 0), (0, 126)))
    (shard,) = run(
        pack_kernel, "pack", (packed_proj, mixer_proj, expand_proj, reduce_proj, gains),
        (arr((8, W_COLS), bf16),), [pltpu.VMEM((3, 8, CHUNKS * CW), f32)],
    )
    weights = lax.all_gather(shard, ALL, axis=0, tiled=True)
    perms = [row_order(order) for order in ORDERS]
    block_output, input_grad, ff, att = local_step(
        tokens, cotangent, sequence_lengths, weights, perms, PartSum
    )
    return (block_output, input_grad, *own_rows(*summed(ff, att)))


def solution(mesh):
    torus = Mesh(mesh.devices.reshape(4, 4, 4, 2), ALL)
    row, flat = P(ALL, None), P(ALL)
    return jax.shard_map(
        body,
        mesh=torus,
        in_specs=(row,) * 5 + (flat, flat, flat, row),
        out_specs=(row,) * 6 + (flat, flat),
        check_vma=False,
    )
```

```python
import functools

import jax
import jax.numpy as jnp
from jax import lax
from jax.experimental import pallas as pl
from jax.experimental.pallas import tpu as pltpu
from jax.sharding import Mesh
from jax.sharding import PartitionSpec as P

H = 16
HD = 64
PAIR = 2 * HD
PAIRS = H // 2
epsilon = 1e-05
rope_base = 160000.0
masked_score = -1e30
AXES = ("y", "z", "x")
ALL = ("y", "z", "x", "c")
VMEM = 60 * 1024 * 1024
bf16 = jnp.bfloat16
f32 = jnp.float32

D = 1024
FF = 2624
CHUNKS = 3
CW = 896
MIX_AT = 3 * D
GAIN_AT = 4 * D
FF_AT = 4 * D + 128
W_COLS = FF_AT + CHUNKS * 3 * CW
ROWS = 512
MIX_CUTS = ((0, 384), (384, 768), (768, 1024))
A_COLS = D + 384


def dot(a, b):
    return lax.dot_general(a, b, (((1,), (0,)), ((), ())), preferred_element_type=f32)


def dot_t(a, b):
    return lax.dot_general(a, b, (((1,), (1,)), ((), ())), preferred_element_type=f32)


def dot_first(a, b):
    return lax.dot_general(a, b, (((0,), (0,)), ((), ())), preferred_element_type=f32)


def norm_parts(values):
    centered = values - jnp.mean(values, axis=-1, keepdims=True)
    scale = lax.rsqrt(jnp.mean(centered * centered, axis=-1, keepdims=True) + epsilon)
    return centered * scale, scale


def half_swapped(v, low_half):
    return jnp.where(low_half, pltpu.roll(v, PAIR - HD // 2, 1), pltpu.roll(v, HD // 2, 1))


def pair_slice(p, at=0):
    return pl.ds(p * PAIR + at, PAIR)


def cotangent_kernel(cot_ref, seg_ref, *refs):
    perms, gt_ref, gtts = refs[:CHUNKS], refs[CHUNKS], refs[CHUNKS + 1 :]
    gt = jnp.where(seg_ref[...] < 4, cot_ref[...].astype(f32), 0.0).astype(bf16)
    gt_ref[...] = gt
    for perm, gtt in zip(perms, gtts):
        gtt[...] = dot_t(perm[...], gt).astype(bf16)


def attend_kernel(
    tok_ref, seg_ref, segt_ref, cos_ref, sin_ref, w_ref,
    qkv_hbm, prob_hbm, res_ref, h1_ref, h2_ref, mixed, gain_ref,
    wp, wm, wg, packed, bias, qkv, prob, sems, out_sems,
):
    copies = [
        pltpu.make_async_copy(w_ref.at[:, pl.ds(GAIN_AT, 128)], wg, sems.at[0]),
        pltpu.make_async_copy(w_ref.at[:, pl.ds(0, 3 * D)], wp, sems.at[1]),
        pltpu.make_async_copy(w_ref.at[:, pl.ds(MIX_AT, D)], wm, sems.at[2]),
    ]
    for c in copies:
        c.start()
    tokens = tok_ref[...].astype(f32)
    xhat, _ = norm_parts(tokens)
    bias[...] = jnp.where(seg_ref[...] == segt_ref[...], 0.0, masked_score)
    copies[0].wait()
    gains = jnp.transpose(wg[...].astype(f32))[:8]
    gain_ref[...] = gains
    h1 = (xhat * gains[0:1]).astype(bf16)
    h1_ref[...] = h1
    copies[1].wait()
    packed[...] = dot(h1, wp[...])
    low_half = lax.broadcasted_iota(jnp.int32, (1, PAIR), 1) % HD < HD // 2
    first = lax.broadcasted_iota(jnp.int32, (1, PAIR), 1) < HD
    zero = jnp.zeros((), bf16)

    def pair(p):
        cos, sin = cos_ref[...], sin_ref[...]
        q = packed[:, pair_slice(p)]
        k = packed[:, pair_slice(p, D)]
        q = (q * cos + half_swapped(q, low_half) * sin).astype(bf16)
        k = (k * cos + half_swapped(k, low_half) * sin).astype(bf16)
        v = packed[:, pair_slice(p, 2 * D)].astype(bf16)
        qkv[:, pair_slice(p)] = q
        qkv[:, pair_slice(p, D)] = k
        qkv[:, pair_slice(p, 2 * D)] = v
        outs = []
        for side in range(2):
            mine = first if side == 0 else jnp.logical_not(first)
            scores = dot_t(jnp.where(mine, q, zero), k) * (HD**-0.5) + bias[...]
            top = jnp.max(scores, axis=-1, keepdims=True)
            e = jnp.exp(scores - top)
            probs = e * (1.0 / jnp.sum(e, axis=-1, keepdims=True))
            prob[2 * p + side] = probs
            outs.append(dot(probs.astype(bf16), v))
        mixed[:, pair_slice(p)] = jnp.where(first, outs[0], outs[1]).astype(bf16)

    outs = []
    for i in range(2):
        for p in range(i * PAIRS // 2, (i + 1) * PAIRS // 2):
            pair(p)
        part = pl.ds(i * PAIRS, PAIRS)
        outs.append(pltpu.make_async_copy(prob.at[part], prob_hbm.at[part], out_sems.at[i]))
        outs[-1].start()
    outs.append(pltpu.make_async_copy(qkv, qkv_hbm, out_sems.at[2]))
    outs[-1].start()
    copies[2].wait()
    residual = tokens + dot(mixed[...], wm[...])
    res_ref[...] = residual
    xhat2, _ = norm_parts(residual)
    h2_ref[...] = (xhat2 * gains[1:2]).astype(bf16)
    for c in outs:
        c.wait()


def started(pairs, sems):
    copies = [pltpu.make_async_copy(a, b, sems.at[i]) for i, (a, b) in enumerate(pairs)]
    for c in copies:
        c.start()
    return copies


def in_part_order(order_ref, part, rows, tmp):
    for r in range(D // 8):
        at = pl.multiple_of(order_ref[part * (D // 8) + r], 8)
        tmp[pl.ds(8 * r, 8), :] = rows[pl.ds(at, 8), :]
    return tmp[...].astype(bf16)


def gated_kernel(
    order_ref, h2_hbm, gt_hbm, gtt0, gtt1, gtt2, w_hbm,
    branch_ref, gh2_ref, sib0, sib1, sib2, own0, own1, own2,
    h2, gt, gtt, w, gate, up, gh, hid, gg, gu, turned, tmp, h2t, grads, sems, out_sems,
):
    pairs = [(h2_hbm, h2)]
    for j, g in enumerate((gtt0, gtt1, gtt2)):
        base = FF_AT + j * 3 * CW
        pairs += [
            (w_hbm.at[:, pl.ds(base + i * CW, CW)], w.at[j, :, pl.ds(i * CW, CW)]) for i in range(3)
        ]
        pairs.append((g, gtt.at[j]))
        if j == 0:
            pairs.append((gt_hbm, gt))
    copies = iter(started(pairs, sems))
    next(copies).wait()
    size = 16

    def rows(i, carry):
        r = pl.ds(pl.multiple_of(i * size, size), size)
        g, u, d = gate[r, :], up[r, :], gh[r, :]
        cdf = 0.5 * (1.0 + lax.erf(g * (0.5**0.5)))
        act = g * cdf
        slope = cdf + g * (jnp.exp(-0.5 * g * g) * 0.3989422804014327)
        hid[r, :] = (act * u).astype(bf16)
        gg[r, :] = (d * u * slope).astype(bf16)
        gu[r, :] = (d * act).astype(bf16)
        return carry

    outs = []
    for j, targets in enumerate(((sib0, own0), (sib1, own1), (sib2, own2))):
        next(copies).wait()
        gate[...] = dot(h2[...], w[j, :, :CW])
        next(copies).wait()
        up[...] = dot(h2[...], w[j, :, CW : 2 * CW])
        for _ in range(3 if j == 0 else 2):
            next(copies).wait()
        gh[...] = dot(gt[...], w[j, :, 2 * CW :])
        if j == 0:
            turned[...] = jnp.transpose(h2[...].astype(f32))
        h2t[...] = in_part_order(order_ref, j, turned, tmp)
        lax.fori_loop(0, gate.shape[0] // size, rows, 0)
        for half, to in enumerate(targets):
            rows_at = pl.ds(half * ROWS, ROWS)
            for i, (left, right) in enumerate(((h2t, gg), (h2t, gu), (gtt.at[j], hid))):
                cols = pl.ds(i * CW, CW)
                grads[j, rows_at, cols] = dot(left[rows_at, :], right[...]).astype(bf16)
                outs.append(
                    pltpu.make_async_copy(
                        grads.at[j, rows_at, cols], to.at[:, cols], out_sems.at[6 * j + 3 * half + i]
                    )
                )
                outs[-1].start()
        more = dot_t(hid[...], w[j, :, 2 * CW :])
        more_gh2 = dot_t(gg[...], w[j, :, :CW]) + dot_t(gu[...], w[j, :, CW : 2 * CW])
        branch_ref[...] = more if j == 0 else branch_ref[...] + more
        gh2_ref[...] = more_gh2 if j == 0 else gh2_ref[...] + more_gh2
    for c in outs:
        c.wait()


def back_kernel(
    gain_ref, seg_ref, cos_ref, sin_ref, gt_ref, res_hbm, branch_hbm, gh2_hbm, qkv_hbm, prob_hbm,
    h1_hbm, mixed_hbm, tok_hbm, w_hbm, order_ref,
    out_ref, gin_ref, sib0, sib1, sib2, own0, own1, own2,
    res_ref, branch_ref, gh2_ref, qkv, prob, h1, mixed, tok, wp, wm,
    gr, ga_ref, gm, gp, h1_turned, mixed_turned, gains_turned, tmp, gains_tmp,
    h1t, mt, grads, sems, out_sems,
):
    copies = started(
        [
            (res_hbm, res_ref), (branch_hbm, branch_ref), (gh2_hbm, gh2_ref),
            (w_hbm.at[:, pl.ds(MIX_AT, D)], wm), (qkv_hbm, qkv), (prob_hbm, prob),
            (h1_hbm, h1), (mixed_hbm, mixed),
            (w_hbm.at[:, pl.ds(0, 3 * D)], wp), (tok_hbm, tok),
        ],
        sems,
    )
    for c in copies[:3]:
        c.wait()
    residual = res_ref[...]
    live = seg_ref[...] < 4
    out_ref[...] = jnp.where(live, residual + branch_ref[...], 0.0).astype(bf16)
    xhat2, r2 = norm_parts(residual)
    gh2 = gh2_ref[...]
    second = jnp.sum(gh2 * xhat2, axis=0, keepdims=True)
    n = gh2 * gain_ref[1:2]
    spread = jnp.mean(n * xhat2, axis=-1, keepdims=True)
    grad_res = gt_ref[...].astype(f32) + r2 * (
        n - jnp.mean(n, axis=-1, keepdims=True) - xhat2 * spread
    )
    gr[...] = grad_res
    ga = grad_res.astype(bf16)
    ga_ref[...] = ga
    copies[3].wait()
    gm[...] = dot_t(ga, wm[...]).astype(bf16)
    copies[4].wait()
    copies[5].wait()
    low_half = lax.broadcasted_iota(jnp.int32, (1, PAIR), 1) % HD < HD // 2
    first = lax.broadcasted_iota(jnp.int32, (1, PAIR), 1) < HD
    zero = jnp.zeros((), bf16)

    def pair(p):
        cos, sin = cos_ref[...], sin_ref[...]
        q = qkv[:, pair_slice(p)]
        k = qkv[:, pair_slice(p, D)]
        v = qkv[:, pair_slice(p, 2 * D)]
        g = gm[:, pair_slice(p)]
        dq, dk, dv = [], [], []
        for side in range(2):
            mine = first if side == 0 else jnp.logical_not(first)
            probs = prob[2 * p + side]
            grad_probs = dot_t(jnp.where(mine, g, zero), v)
            weighted = probs * grad_probs
            delta = jnp.sum(weighted, axis=-1, keepdims=True)
            gs = (weighted - probs * delta).astype(bf16)
            dq.append(dot(gs, k))
            dk.append(dot_first(gs, q))
            dv.append(dot_first(probs.astype(bf16), g))
        dq = jnp.where(first, dq[0], dq[1]) * (HD**-0.5)
        dk = jnp.where(first, dk[0], dk[1]) * (HD**-0.5)
        dv = jnp.where(first, dv[0], dv[1])
        gp[:, pair_slice(p)] = (dq * cos - half_swapped(dq, low_half) * sin).astype(bf16)
        gp[:, pair_slice(p, D)] = (dk * cos - half_swapped(dk, low_half) * sin).astype(bf16)
        gp[:, pair_slice(p, 2 * D)] = dv.astype(bf16)

    for p in range(PAIRS):
        pair(p)
    copies[6].wait()
    copies[7].wait()
    h1_turned[...] = jnp.transpose(h1[...].astype(f32))
    mixed_turned[...] = jnp.transpose(mixed[...].astype(f32))
    outs = []
    for j in range(CHUNKS):
        h1t[...] = in_part_order(order_ref, j, h1_turned, tmp)
        mt[...] = in_part_order(order_ref, j, mixed_turned, tmp)
        lo, hi = MIX_CUTS[j]
        to = grads.at[j]
        to[:, pl.ds(0, D)] = dot(h1t[...], gp[:, j * D : (j + 1) * D]).astype(bf16)
        to[:, pl.ds(D, hi - lo)] = dot(mt[...], ga_ref[:, lo:hi]).astype(bf16)
        if j == CHUNKS - 1:
            copies[8].wait()
            copies[9].wait()
            gh1 = dot_t(gp[...], wp[...])
            xhat1, r1 = norm_parts(tok[...].astype(f32))
            one = jnp.sum(gh1 * xhat1, axis=0, keepdims=True)
            m = gh1 * gain_ref[0:1]
            spread = jnp.mean(m * xhat1, axis=-1, keepdims=True)
            gin_ref[...] = gr[...] + r1 * (m - jnp.mean(m, axis=-1, keepdims=True) - xhat1 * spread)
            row = lax.broadcasted_iota(jnp.int32, (128, D), 0)
            both = jnp.where(row == 0, one, jnp.where(row == 1, second, 0.0))
            gains_turned[...] = jnp.transpose(both)
            to[:, pl.ds(D + 256, 128)] = in_part_order(order_ref, j, gains_turned, gains_tmp)
        for half, group in enumerate(((sib0, sib1, sib2), (own0, own1, own2))):
            outs.append(
                pltpu.make_async_copy(
                    grads.at[j, pl.ds(half * ROWS, ROWS)], group[j], out_sems.at[2 * j + half]
                )
            )
            outs[-1].start()
    for c in outs:
        c.wait()


def turn_kernel(ff_terms, *refs):
    send, keep, whole = refs[ff_terms + 4 :]
    at = 0
    for terms in (refs[:ff_terms], refs[ff_terms : ff_terms + 4]):
        total = terms[0][...].astype(f32)
        for t in terms[1:]:
            total = total + t[...].astype(f32)
        whole[:, pl.ds(at, total.shape[1])] = total
        at += total.shape[1]
    send[...] = whole[pl.ds(0, 64), :].astype(bf16)
    keep[...] = whole[pl.ds(64, 64), :].astype(bf16)


def pack_kernel(packed, mixer, expand, reduce, gains, out, wide):
    out[:, pl.ds(0, MIX_AT)] = packed[...]
    out[:, pl.ds(MIX_AT, D)] = mixer[...]
    out[:, pl.ds(GAIN_AT, 128)] = gains[...]
    both = expand[...].astype(f32)
    wide[...] = jnp.zeros(wide.shape, f32)
    wide[0, :, pl.ds(0, FF)] = both[:, :FF]
    wide[1, :, pl.ds(0, FF)] = pltpu.roll(both, FF, 1)[:, :FF]
    wide[2, :, pl.ds(0, FF)] = reduce[...].astype(f32)
    for j in range(CHUNKS):
        for i in range(3):
            out[:, pl.ds(FF_AT + (3 * j + i) * CW, CW)] = wide[i, :, pl.ds(j * CW, CW)].astype(bf16)


def finish_kernel(*refs):
    gots, kepts = refs[:3], refs[3:6]
    packed, mixer, expand, reduce, gain, wide = refs[6:]
    ff = 3 * CW
    for j in range(CHUNKS):
        total = gots[j][...].astype(f32) + kepts[j][...].astype(f32)
        for i in range(3):
            wide[i, :, pl.ds(j * CW, CW)] = total[:, i * CW : (i + 1) * CW]
        packed[:, pl.ds(j * D, D)] = total[:, ff : ff + D]
        lo, hi = MIX_CUTS[j]
        mixer[:, pl.ds(lo, hi - lo)] = total[:, ff + D : ff + D + hi - lo]
    gain[...] = jnp.transpose(total[:, ff + D + 256 :])[:8]
    reduce[...] = wide[2, :, pl.ds(0, FF)]
    lane = lax.broadcasted_iota(jnp.int32, (1, 2 * FF), 1)
    pad = jnp.zeros((8, 2 * FF - CHUNKS * CW), f32)
    gate = jnp.concatenate([wide[0], pad], axis=1)
    up = pltpu.roll(jnp.concatenate([wide[1], pad], axis=1), FF, 1)
    expand[...] = jnp.where(lane < FF, gate, up)


def arr(shape, dtype):
    return jax.ShapeDtypeStruct(shape, dtype)


VSPEC = pl.BlockSpec(memory_space=pltpu.VMEM)
HSPEC = pl.BlockSpec(memory_space=pl.ANY)
SSPEC = pl.BlockSpec(memory_space=pltpu.SMEM)
DMA = pltpu.SemaphoreType.DMA


def run(
    kernel, name, inputs, out_shape, scratch=(), in_hbm=(), out_hbm=(), after=(), through=(), specs=(),
    in_smem=(),
):
    count, outs, extra = len(inputs), len(out_shape), len(after) + len(through)

    def with_order(*refs):
        rest = refs[count + extra :]
        kernel(*refs[:count], *rest[:outs], *rest[outs + len(through) :])

    return pl.pallas_call(
        with_order,
        out_shape=tuple(out_shape) + tuple(arr(t.shape, t.dtype) for t in through),
        grid=(1,) if specs else (),
        in_specs=(
            list(specs)
            or [HSPEC if i in in_hbm else SSPEC if i in in_smem else VSPEC for i in range(count)]
        )
        + [HSPEC] * extra,
        out_specs=tuple(HSPEC if i in out_hbm else VSPEC for i in range(outs))
        + (HSPEC,) * len(through),
        input_output_aliases={count + len(after) + i: outs + i for i in range(len(through))},
        scratch_shapes=list(scratch),
        compiler_params=pltpu.CompilerParams(vmem_limit_bytes=VMEM),
        cost_estimate=pl.CostEstimate(flops=10**14, bytes_accessed=1024, transcendentals=0),
        name=name,
    )(*inputs, *after, *through)


def token_layout(lengths, slot_count):
    places = jnp.arange(slot_count, dtype=jnp.int32)
    ends = jnp.cumsum(lengths)
    starts = ends - lengths
    segment = jnp.sum((places[:, None] >= ends[None, :]).astype(jnp.int32), axis=1)
    live = places < ends[-1]
    picked = (segment[:, None] == jnp.arange(lengths.shape[0], dtype=jnp.int32)[None, :]).astype(
        jnp.int32
    )
    position = jnp.where(live, places - jnp.sum(picked * starts[None, :], axis=1), 0)
    segment = jnp.where(live, segment, lengths.shape[0] + places)
    return segment, position


def rotary_tables(position):
    frequency = rope_base ** (-(jnp.arange(HD // 2, dtype=f32) * 2.0 / HD))
    angles = position.astype(f32)[:, None] * frequency
    cos, sin = jnp.cos(angles), jnp.sin(angles)
    return (
        jnp.concatenate([cos, cos, cos, cos], axis=-1),
        jnp.concatenate([-sin, sin, -sin, sin], axis=-1),
    )


ORDERS = (("x", "y", "z"), ("y", "z", "x"), ("z", "x", "y"))


def hops(core):
    return (1, 3) if core == 0 else (3, 1)


def row_features(order, swapped=False):
    core = lax.axis_index("c")
    row = jnp.arange(D, dtype=jnp.int32)
    mine, inner = row >= ROWS, row % ROWS
    side = jnp.where(mine, core, 1 - core)
    place = {}
    for axis, size in zip(order, (128, 32, 8)):
        turn = inner // size % 4
        low = side == (1 if swapped and axis == order[0] else 0)
        apart = jnp.where(turn == 0, 2, jnp.where(turn == 3, 0, jnp.where((turn == 1) == low, 1, 3)))
        place[axis] = lax.axis_index(axis) ^ apart
    return ((place["y"] * 4 + place["z"]) * 4 + place["x"]) * 16 + side * 8 + inner % 8


def row_order(order):
    return (row_features(order)[:, None] == jnp.arange(D, dtype=jnp.int32)[None, :]).astype(bf16)


def to_partner(a, axis, step, swapped=0):
    pairs = [(i * 2 + c, (i ^ hops(c ^ swapped)[step]) * 2 + c) for i in range(4) for c in range(2)]
    return lax.ppermute(a, (axis, "c"), pairs)


def to_sibling(a):
    return lax.ppermute(a, "c", [(0, 1), (1, 0)])


def added(*arrays):
    total = arrays[0]
    for a in arrays[1:]:
        total = total + a
    return total


class PartSum:
    def __init__(self, order, sib, own, swapped=0):
        self.axis, self.swapped = order[0], swapped
        self.own, self.arrived = own, to_sibling(sib)
        self.lo, self.step, self.got = 0, 0, None

    def piece(self, lo, rows):
        at = slice(lo, lo + rows)
        terms = [self.own[at], self.arrived[at]]
        if self.got is not None:
            terms.append(self.got[lo - self.lo : lo - self.lo + rows])
        return added(*terms)

    def send(self):
        rows = (ROWS - self.lo) // 2
        out = self.piece(self.lo, rows)
        got = to_partner(out, self.axis, self.step, self.swapped)
        self.got = got if self.got is None else (got, self.got)
        self.lo += rows
        self.step += 1
        return out

    def last_terms(self):
        cols = self.own.shape[1]
        got, kept = self.got
        specs = [pl.BlockSpec((128, cols), lambda i, at=at: (at, 0)) for at in (3, 3, 0, 1)]
        return (self.own, self.arrived, got, kept), specs

    def total(self):
        got, kept = self.got
        at = slice(self.lo, ROWS)
        return (added(self.own[at], self.arrived[at], got, kept[ROWS // 4 :]),), [VSPEC]


def halves(a):
    n = a.shape[0] // 2
    return a[:n], a[n:]


def local_step(tokens, cotangent, lengths, weights, perms, part_sum):
    n = tokens.shape[0]
    segment, position = token_layout(lengths, n)
    cos, sin = rotary_tables(position)
    seg_col, seg_row = segment[:, None], segment[None, :]
    tile = arr((n, D), bf16)
    wide = arr((n, D), f32)
    vm = pltpu.VMEM
    orders = jnp.concatenate([row_features(order)[::8] for order in ORDERS])
    att_orders = jnp.concatenate([row_features(order, True)[::8] for order in ORDERS])
    gt, *gtts = run(
        cotangent_kernel, "cotangent", (cotangent, seg_col, *perms),
        (tile,) + (arr((D, n), bf16),) * CHUNKS,
    )
    qkv, probs, residual, h1, h2, mixed, gains = run(
        attend_kernel, "attend", (tokens, seg_col, seg_row, cos, sin, weights),
        (arr((n, 3 * D), bf16), arr((H, n, n), f32), wide, tile, tile, tile, arr((8, D), f32)),
        [
            vm((D, 3 * D), bf16), vm((D, D), bf16), vm((D, 128), bf16), vm((n, 3 * D), f32),
            vm((n, n), f32), vm((n, 3 * D), bf16), vm((H, n, n), f32), DMA((3,)), DMA((3,)),
        ],
        in_hbm=(5,),
        out_hbm=(0, 1),
    )
    branch, gh2, *pieces = run(
        gated_kernel, "gated", (orders, h2, gt, *gtts, weights),
        (wide, wide) + (arr((ROWS, 3 * CW), bf16),) * 6,
        [vm((n, D), bf16), vm((n, D), bf16), vm((3, D, n), bf16)]
        + [vm((3, D, 3 * CW), bf16)]
        + [vm((n, CW), f32)] * 3
        + [vm((n, CW), bf16)] * 3
        + [vm((D, n), f32), vm((D, n), f32)]
        + [vm((D, n), bf16), vm((3, D, 3 * CW), bf16), DMA((14,)), DMA((18,))],
        in_hbm=range(1, 7),
        in_smem=(0,),
        out_hbm=range(2, 8),
    )
    ff = [part_sum(ORDERS[j], pieces[j], pieces[3 + j]) for j in range(CHUNKS)]
    after = ()
    for f in ff:
        if after:
            f.own, _ = lax.optimization_barrier((f.own, after[-1]))
        after += (f.send(),)
    block_output, input_grad, *pieces = run(
        back_kernel, "back",
        (gains, seg_col, cos, sin, gt, residual, branch, gh2, qkv, probs, h1, mixed, tokens, weights, att_orders),
        (tile, wide) + (arr((ROWS, A_COLS), bf16),) * 6,
        [vm((n, D), f32)] * 3
        + [vm((n, 3 * D), bf16), vm((H, n, n), f32)]
        + [vm((n, D), bf16)] * 3
        + [vm((D, 3 * D), bf16), vm((D, D), bf16), vm((n, D), f32), vm((n, D), bf16), vm((n, D), bf16)]
        + [vm((n, 3 * D), bf16), vm((D, n), f32), vm((D, n), f32), vm((D, 128), f32), vm((D, n), f32)]
        + [vm((D, 128), f32), vm((D, n), bf16), vm((D, n), bf16), vm((3, D, A_COLS), bf16)]
        + [DMA((10,)), DMA((6,))],
        in_hbm=range(5, 14),
        in_smem=(14,),
        out_hbm=range(2, 8),
        after=after,
        through=tuple(f.own for f in ff),
    )
    for f, own in zip(ff, pieces[6:]):
        f.own = own
    att = [part_sum(ORDERS[j], pieces[j], pieces[3 + j], 1) for j in range(CHUNKS)]
    return block_output, input_grad, ff, att


def summed(ff, att):
    for f in ff:
        f.send()
    for f, a in zip(ff, att):
        f.own, _ = lax.optimization_barrier((f.own, a.send()))
    for a in att:
        a.send()
    pairs = []
    for f, a in zip(ff, att):
        f_terms, f_specs = f.total()
        a_terms, a_specs = a.last_terms()
        cols = f.own.shape[1] + a.own.shape[1]
        pairs.append(
            run(
                functools.partial(turn_kernel, len(f_terms)), "turn", f_terms + a_terms, (arr((64, cols), bf16),) * 2,
                [pltpu.VMEM((128, cols), f32)], specs=f_specs + a_specs,
            )
        )
    for ring, step in ((1, 0), (1, 1), (2, 0), (2, 1)):
        gots = [to_partner(p[0], order[ring], step) for p, order in zip(pairs, ORDERS)]
        kept = [p[1] for p in pairs]
        if (ring, step) != (2, 1):
            pairs = [halves(added(g, k)) for g, k in zip(gots, kept)]
    return gots, kept


def own_rows(gots, kept):
    n = 8
    *grads, gains = run(
        finish_kernel, "finish", (*gots, *kept),
        tuple(arr((n, c), f32) for c in (3 * D, D, 2 * FF, FF, 8)),
        [pltpu.VMEM((3, n, CHUNKS * CW), f32)],
    )
    return (*grads, gains[0], gains[1])


def body(
    tokens, packed_proj, mixer_proj, expand_proj, reduce_proj, first_gain, second_gain,
    sequence_lengths, cotangent,
):
    gains = jnp.pad(jnp.stack([first_gain, second_gain], axis=1), ((0, 0), (0, 126)))
    (shard,) = run(
        pack_kernel, "pack", (packed_proj, mixer_proj, expand_proj, reduce_proj, gains),
        (arr((8, W_COLS), bf16),), [pltpu.VMEM((3, 8, CHUNKS * CW), f32)],
    )
    weights = lax.all_gather(shard, ALL, axis=0, tiled=True)
    perms = [row_order(order) for order in ORDERS]
    block_output, input_grad, ff, att = local_step(
        tokens, cotangent, sequence_lengths, weights, perms, PartSum
    )
    return (block_output, input_grad, *own_rows(*summed(ff, att)))


def solution(mesh):
    torus = Mesh(mesh.devices.reshape(4, 4, 4, 2), ALL)
    row, flat = P(ALL, None), P(ALL)
    return jax.shard_map(
        body,
        mesh=torus,
        in_specs=(row,) * 5 + (flat, flat, flat, row),
        out_specs=(row,) * 6 + (flat, flat),
        check_vma=False,
    )
```
